768 devices in a mesh: slab: 96 (over z_lo, y, core), angle: 8 (over x, z_hi).
Axes of the slice: x: 4, y: 8, z: 12 (z_hi: 2, z_lo: 6; z = z_hi * 6 + z_lo), core: 2. Of those that a mesh axis runs over, the one named last changes fastest.
Arguments:
- volume: float32 [1024, 768, 128], P('angle', 'slab'), may hold values from -6 to 6
- dual: float32 [8, 768, 4096], P('angle', 'slab'), may hold values from -6 to 6
- measured: float32 [8, 768, 4096], P('angle', 'slab'), may hold values from -6 to 6
- tiles: bfloat16 [64, 128, 128], replicated, may hold values from -0.09375 to 0.09375
- lists: int32 [3, 96, 8192], P(None, 'slab', 'angle'), may hold values from 0 to 1023, as said below
- live: int32 [96, 64], P('slab', 'angle'), may hold values from 0 to 128, as said below
- dual_kernel: float32 [2, 3], replicated, may hold values from -1 to 1
- primal_kernel: float32 [2, 3], replicated, may hold values from -1 to 1
Outputs:
- new_volume: float32 [1024, 768, 128], P('angle', 'slab')
- new_dual: float32 [8, 768, 4096], P('angle', 'slab')
The draws below stay inside these ranges and needn't reach their ends.
Inputs may be any that keep to these rules, and one draw needn't show every extreme that they name: Row 0 of lists: position p of a list lies in segment j = (p % 1024) // 128 and names a voxel block of j*128 to (j+1)*128 - 1. Row 1 names a detector block 0 to 31 of the list's own angle group; row 2 a tile 0 to 63. live[s, g*8 + j] counts the live leading positions of segment j of the list of slab s and angle group g.
All inputs are finite; a program needn't handle non-finite values.
Results may differ from the reference program's by a relative error of at most 0.0015.
Values may be sent and summed in bfloat16 or wider, within the bound.
A program may use at most 32 MiB of HBM per device.

```python
import jax
import jax.numpy as jnp
from jax import lax

ROWS = 8
VB_DEV = 128
ANG_DEV = 1
NNZ = 1024
U = 4096
BLK = 128
NT = 64
UB = 32
NVB = 1024
ANGLES = 8
NZ = 768
N_SLAB = 96
N_ANGLE = 8


def draw_lists(key, part):
    key = jax.random.fold_in(key, 11)
    seg_len = NNZ // N_ANGLE
    key_vox, key_det, key_tile = jax.random.split(key, 3)
    positions = jnp.arange(N_ANGLE * NNZ, dtype=jnp.int32) % NNZ
    segment = (positions // seg_len)[None, :]
    inside = (positions % seg_len)[None, :]
    offset = jax.random.randint(key_vox, (N_SLAB, N_ANGLE * NNZ), 0, VB_DEV, dtype=jnp.int32)
    offset = jnp.where(inside == 0, VB_DEV - 1, offset)
    offset = jnp.where(inside == 1, 0, offset)
    voxels = segment * VB_DEV + offset
    detector = jax.random.randint(key_det, (N_SLAB, N_ANGLE * NNZ), 0, ANG_DEV * UB, dtype=jnp.int32)
    tile_ids = jax.random.randint(key_tile, (N_SLAB, N_ANGLE * NNZ), 0, NT, dtype=jnp.int32)
    return jnp.stack([voxels, detector, tile_ids]).astype(jnp.int32)


def draw_live(key, part):
    key = jax.random.fold_in(key, 12)
    seg_len = NNZ // N_ANGLE
    slab_idx = jnp.arange(N_SLAB, dtype=jnp.int32)[:, None]
    column = jnp.arange(N_ANGLE * N_ANGLE, dtype=jnp.int32)[None, :]
    profile = N_SLAB - jnp.abs(2 * slab_idx + 1 - N_SLAB) + 1
    base = seg_len // 4 + (seg_len - seg_len // 4) * profile // N_SLAB
    jitter = jax.random.randint(key, (N_SLAB, N_ANGLE * N_ANGLE), 0, seg_len // 4 + 1, dtype=jnp.int32)
    counts = base - jitter
    counts = jnp.where((slab_idx == N_SLAB // 2) & (column == 0), seg_len, counts)
    return counts.astype(jnp.int32)


def shard_levels(key, shape, cuts, least, high):
    factor_of, own = 1.0, jax.random.fold_in(key, 6)
    for position, blocks in cuts:
        steps = jnp.exp(jax.random.uniform(jax.random.fold_in(own, position), (blocks,), jnp.float32, least / len(cuts), high / len(cuts)))
        factor_of = factor_of * jnp.repeat(steps, shape[position] // blocks).reshape([-1 if axis == position else 1 for axis in range(len(shape))])
    return factor_of


def scatter_about(stream_key, dims, spread, bound, shards=(), kind=jnp.bfloat16):
    drawn = jax.random.normal(stream_key, dims, jnp.float32) * spread
    if len(shards) > 0:
        drawn = shard_levels(stream_key, dims, shards, -0.22, 0.18) * drawn
    return jnp.clip(drawn, min=-bound, max=bound).astype(kind)


def setup_inputs(seed: int = 0) -> dict:
    key_of = jax.random.split(jax.random.key(seed), 9)
    volume = scatter_about(key_of[0], (NVB, NZ, BLK), 1.0, 6.0, ((0, 8), (1, 96)), jnp.float32)
    dual = scatter_about(key_of[1], (ANGLES, NZ, U), 1.0, 6.0, ((0, 8), (1, 96)), jnp.float32)
    measured = scatter_about(key_of[2], (ANGLES, NZ, U), 1.0, 6.0, ((0, 8), (1, 96)), jnp.float32)
    tiles = scatter_about(key_of[3], (NT, BLK, BLK), (BLK * NNZ // (ANG_DEV * UB)) ** -0.5, 0.09375)
    lists = draw_lists(jax.random.fold_in(key_of[8], 71), 0)
    live = draw_live(jax.random.fold_in(key_of[8], 71), 0)
    dual_kernel = jnp.clip(jax.random.uniform(key_of[6], (2, 3), jnp.float32, -1.0, 1.0), -1.0, 1.0)
    primal_kernel = jnp.clip(jax.random.uniform(key_of[7], (2, 3), jnp.float32, -1.0, 1.0), -1.0, 1.0)
    return {"volume": volume, "dual": dual, "measured": measured, "tiles": tiles, "lists": lists, "live": live, "dual_kernel": dual_kernel, "primal_kernel": primal_kernel}


def row_conv(first, second, kernel):
    count_rows = first.shape[1]
    first_pad = jnp.pad(first, ((0, 0), (1, 1), (0, 0)))
    second_pad = jnp.pad(second, ((0, 0), (1, 1), (0, 0)))
    summed = jnp.zeros_like(first)
    for shift_idx in range(3):
        summed = summed + kernel[0, shift_idx] * first_pad[:, shift_idx:shift_idx + count_rows]
        summed = summed + kernel[1, shift_idx] * second_pad[:, shift_idx:shift_idx + count_rows]
    return summed


def pair_entries(lists, live, slab_idx, group_idx):
    seg_len = NNZ // N_ANGLE
    positions = jnp.arange(NNZ, dtype=jnp.int32)
    chosen = lax.dynamic_slice(lists, (jnp.int32(0), slab_idx, group_idx * NNZ), (3, 1, NNZ))[:, 0]
    counts = lax.dynamic_slice(live, (slab_idx, group_idx * N_ANGLE), (1, N_ANGLE))[0]
    alive_mask = (positions % seg_len < counts[positions // seg_len]).astype(jnp.float32)
    return chosen, alive_mask


def reference(volume, dual, measured, tiles, lists, live, dual_kernel, primal_kernel):
    det_blocks = ANG_DEV * UB
    rounded = lax.optimization_barrier(volume.astype(jnp.bfloat16)).astype(jnp.float32)
    tiles_wide = tiles.astype(jnp.float32)

    def forward_pair(pair):
        slab_idx = pair // N_ANGLE
        group_idx = pair % N_ANGLE
        chosen, alive_mask = pair_entries(lists, live, slab_idx, group_idx)
        rows_here = lax.dynamic_slice_in_dim(rounded, slab_idx * ROWS, ROWS, 1)
        product = jnp.einsum('erv,edv->erd', rows_here[chosen[0]], tiles_wide[chosen[2]])
        product = product * alive_mask[:, None, None]
        return jax.ops.segment_sum(product, chosen[1], num_segments=det_blocks)

    projected = lax.map(forward_pair, jnp.arange(N_SLAB * N_ANGLE, dtype=jnp.int32))
    projected = projected.reshape(N_SLAB, N_ANGLE, ANG_DEV, UB, ROWS, BLK)
    projected = projected.transpose(1, 2, 0, 4, 3, 5).reshape(ANGLES, NZ, U)
    misfit = projected - measured
    new_dual = dual + row_conv(dual, misfit, dual_kernel)
    ramp = 2.0 * jnp.arange(U // 2 + 1, dtype=jnp.float32) / U
    filtered = jnp.fft.irfft(jnp.fft.rfft(new_dual, axis=-1) * ramp, n=U, axis=-1)
    q_round = lax.optimization_barrier(filtered.astype(jnp.bfloat16)).astype(jnp.float32)
    q_blocks = q_round.reshape(N_ANGLE, ANG_DEV, N_SLAB, ROWS, UB, BLK)
    q_blocks = q_blocks.transpose(2, 0, 1, 4, 3, 5).reshape(N_SLAB, N_ANGLE, det_blocks, ROWS, BLK)

    def back_slab(slab_idx):
        def one_group(accum, group_idx):
            chosen, alive_mask = pair_entries(lists, live, slab_idx, group_idx)
            blocks_here = q_blocks[slab_idx, group_idx]
            product = jnp.einsum('erd,edv->erv', blocks_here[chosen[1]], tiles_wide[chosen[2]])
            product = product * alive_mask[:, None, None]
            return accum + jax.ops.segment_sum(product, chosen[0], num_segments=NVB), None

        start_acc = jnp.zeros((NVB, ROWS, BLK), jnp.float32)
        return lax.scan(one_group, start_acc, jnp.arange(N_ANGLE, dtype=jnp.int32))[0]

    back = lax.map(back_slab, jnp.arange(N_SLAB, dtype=jnp.int32))
    back = back.transpose(1, 0, 2, 3).reshape(NVB, NZ, BLK)
    new_volume = volume + row_conv(volume, back, primal_kernel)
    return new_volume, new_dual
```

```python
import functools

import jax
import jax.numpy as jnp
import ml_dtypes
import numpy as np
from jax import lax
from jax.experimental import pallas as pl
from jax.experimental.pallas import tpu as pltpu
from jax.sharding import PartitionSpec as P

F32 = jnp.float32
BF16 = jnp.bfloat16
MESH = pl.DeviceIdType.MESH
CONTRACT_LAST = (((1,), (1,)), ((), ()))
CONTRACT_INNER = (((1,), (0,)), ((), ()))
VMEM_LIMIT = 56 * 2**20
X_SIZE = 4
CHUNKS = 4


def ramp_matrix(width, blk):
    n = np.arange(width)
    taps = np.zeros(width)
    odd = n % 2 == 1
    taps[odd] = -(2.0 / width**2) / np.sin(np.pi * n[odd] / width) ** 2
    k = np.arange(width // blk)[:, None, None]
    i = np.arange(blk)[None, :, None]
    j = np.arange(blk)[None, None, :]
    full = taps[(blk * k + j - i) % width].reshape(width, blk)
    high = full.astype(ml_dtypes.bfloat16)
    low = (full - high.astype(np.float64)).astype(ml_dtypes.bfloat16)
    return np.concatenate([high, low], axis=1)


def greet(partners, conditional):
    barrier = pltpu.get_barrier_semaphore()
    for partner in partners:
        pl.semaphore_signal(barrier, inc=1, device_id=partner, device_id_type=MESH)
    for present, partner in conditional:

        @pl.when(present)
        def _():
            pl.semaphore_signal(barrier, inc=1, device_id=partner, device_id_type=MESH)

    present_count = sum([present.astype(jnp.int32) for present, _partner in conditional], jnp.int32(len(partners)))
    pl.semaphore_wait(barrier, present_count)


def remote(src, dst, send, recv, device):
    return pltpu.make_async_remote_copy(
        src_ref=src, dst_ref=dst, send_sem=send, recv_sem=recv, device_id=device, device_id_type=MESH
    )


def lists_kernel(groups, in_ref, out_ref, land, send, recv):
    slab, me = lax.axis_index("slab"), lax.axis_index("angle")
    greet([(slab, lax.rem(me + d, groups)) for d in range(1, groups)], [])
    copies = []
    for d in range(1, groups):
        to = lax.rem(me + d, groups)
        copy = remote(in_ref.at[to], land.at[me], send.at[d - 1], recv.at[d - 1], (slab, to))
        copy.start()
        copies.append(copy)
    land[me] = in_ref[me]
    for copy in copies:
        copy.wait()
    out_ref[...] = land[...]


def forward_kernel(idx_ref, vol_ref, tiles_ref, out_ref, dense, rounded, *sums):
    blocks = vol_ref.shape[0]
    groups, rows, blk = out_ref.shape
    tile_count = tiles_ref.shape[0]
    rounded[...] = vol_ref[...].reshape(blocks * 8, blk).astype(BF16)
    for total in sums:
        total[...] = jnp.zeros_like(total)

    def products(i, _):
        pair = tiles_ref[pl.ds(i * 2, 2)].reshape(2 * blk, blk)
        both = lax.dot_general(rounded[...], pair, CONTRACT_LAST, preferred_element_type=F32)
        dense[pl.ds(i * 2 * blocks, blocks)] = both[:, :blk].reshape(blocks, 8, blk)
        dense[pl.ds((i * 2 + 1) * blocks, blocks)] = both[:, blk:].reshape(blocks, 8, blk)
        return 0

    lax.fori_loop(0, tile_count // 2, products, 0)

    def add(i, _):
        for u in range(4):
            for g in range(groups):
                p = i * 4 + u
                sums[g][idx_ref[g, 1, p]] += dense[idx_ref[g, 2, p] * blocks + idx_ref[g, 0, p]]
        return 0

    lax.fori_loop(0, idx_ref.shape[2] // 4, add, 0)
    for g in range(groups):
        out_ref[g] = sums[g][: rows // 8].reshape(rows, blk).astype(BF16)


def backward_kernel(idx_ref, q_ref, tiles_ref, out_ref, wide, spread):
    blocks = out_ref.shape[0]
    groups, rows, blk = q_ref.shape
    det = rows // 8
    tile_count = tiles_ref.shape[0]
    for g in range(groups):
        wide[pl.ds(g * (det + 1), det)] = q_ref[g].reshape(det, 8, blk).astype(F32)
        wide[g * (det + 1) + det] = jnp.zeros((8, blk), F32)

    def clear(i, _):
        spread[pl.ds(i * blocks, blocks)] = jnp.zeros((blocks, 8, blk), F32)
        return 0

    lax.fori_loop(0, tile_count, clear, 0)

    def add(i, _):
        for u in range(2):
            for g in range(groups):
                p = i * 2 + u
                source = wide[idx_ref[g, 1, p] + g * (det + 1)]
                spread[idx_ref[g, 2, p] * blocks + idx_ref[g, 0, p]] += source
        return 0

    lax.fori_loop(0, idx_ref.shape[2] // 2, add, 0)
    out_ref[...] = jnp.zeros_like(out_ref)

    def products(i, _):
        left = spread[pl.ds(i * 2 * blocks, blocks)].reshape(blocks * 8, blk).astype(BF16)
        right = spread[pl.ds((i * 2 + 1) * blocks, blocks)].reshape(blocks * 8, blk).astype(BF16)
        both = jnp.concatenate([left, right], axis=1)
        pair = tiles_ref[pl.ds(i * 2, 2)].reshape(2 * blk, blk)
        added = lax.dot_general(both, pair, CONTRACT_INNER, preferred_element_type=F32)
        out_ref[...] += added.reshape(blocks, 8, blk)
        return 0

    lax.fori_loop(0, tile_count // 2, products, 0)


def dual_kernel_body(
    slabs,
    part_ref,
    dual_ref,
    meas_ref,
    ramp_ref,
    weights,
    new_ref,
    q_ref,
    land_x,
    send_z,
    land_z,
    own,
    misfit,
    down,
    up,
    from_prev,
    from_next,
    even,
    odd,
    even_low,
    odd_low,
    sx,
    rx,
    sz,
    rz,
    se,
    re,
    gx_s,
    gx_r,
    gz_s,
    gz_r,
    fx_s,
    fx_r,
):
    slab, me = lax.axis_index("slab"), lax.axis_index("angle")
    x, z = me // 2, lax.rem(me, 2)
    partner = (slab, 2 * x + 1 - z)
    has_prev, has_next = slab > 0, slab < slabs - 1
    prev, following = (slab - 1, me), (slab + 1, me)
    peers = [lax.rem(x + d, X_SIZE) for d in range(1, X_SIZE)]
    rows, blk = part_ref.shape[1:]
    width = dual_ref.shape[1]
    det = width // blk
    greet([(slab, 2 * t + z) for t in peers] + [partner], [(has_prev, prev), (has_next, following)])

    step = rows // CHUNKS
    x_copies = []
    for c in range(CHUNKS):
        part = pl.ds(c * step, step)
        line = []
        for d, t in enumerate(peers):
            copy = remote(
                part_ref.at[pl.ds(2 * t, 2), part], land_x.at[d, :, part], sx.at[d, c], rx.at[d, c], (slab, 2 * t + z)
            )
            copy.start()
            line.append(copy)
        x_copies.append(line)
    z_copies = []
    for c in range(CHUNKS):
        part = pl.ds(c * step, step)
        for copy in x_copies[c]:
            copy.wait_recv()
        for side in (1, 0):
            k = 1 - z if side else z
            total = part_ref[2 * x + k, part].astype(F32)
            for d in range(X_SIZE - 1):
                total = total + land_x[d, k, part].astype(F32)
            if side:
                send_z[part] = total.astype(BF16)
                copy = remote(send_z.at[part], land_z.at[part], sz.at[c], rz.at[c], partner)
                copy.start()
                z_copies.append(copy)
            else:
                own[part] = total
    for c in range(CHUNKS):
        z_copies[c].wait_recv()
        for b in range(c * step // 8, (c + 1) * step // 8, 2):
            both = own[pl.ds(b * 8, 16)] + land_z[pl.ds(b * 8, 16)].astype(F32)
            cols = pl.ds(b * blk, blk)
            misfit[:, cols] = both[:8] - meas_ref[:, cols]
            cols = pl.ds((b + 1) * blk, blk)
            misfit[:, cols] = both[8:] - meas_ref[:, cols]

    down[...] = weights[0, 0] * dual_ref[7:8, :] + weights[1, 0] * misfit[7:8, :]
    up[...] = weights[0, 2] * dual_ref[0:1, :] + weights[1, 2] * misfit[0:1, :]
    to_next = remote(down, from_prev, se.at[0], re.at[0], following)
    to_prev = remote(up, from_next, se.at[1], re.at[1], prev)

    @pl.when(has_next)
    def _():
        to_next.start()

    @pl.when(has_prev)
    def _():
        to_prev.start()

    @pl.when(has_prev)
    def _():
        to_next.wait_recv()

    @pl.when(jnp.logical_not(has_prev))
    def _():
        from_prev[...] = jnp.zeros_like(from_prev)

    @pl.when(has_next)
    def _():
        to_prev.wait_recv()

    @pl.when(jnp.logical_not(has_next))
    def _():
        from_next[...] = jnp.zeros_like(from_next)

    row = lax.broadcasted_iota(jnp.int32, (8, blk), 0)

    def updated(b):
        cols = pl.ds(b * blk, blk)
        dual, mis = dual_ref[:, cols], misfit[:, cols]
        before = pltpu.roll(weights[0, 0] * dual + weights[1, 0] * mis, 1, 0)
        after = pltpu.roll(weights[0, 2] * dual + weights[1, 2] * mis, 7, 0)
        before = jnp.where(row == 0, from_prev[:, cols], before)
        after = jnp.where(row == 7, from_next[:, cols], after)
        new = dual + weights[0, 1] * dual + weights[1, 1] * mis + before + after
        new_ref[:, cols] = new
        return new

    def split(value):
        high = value.astype(BF16)
        return high, (value - high.astype(F32)).astype(BF16)

    news = [updated(b) for b in range(det)]
    for b in range(det):
        high, low = split(jnp.concatenate([news[b], news[(b + 1) % det]], axis=0))
        if b % 2 == 0:
            for base in (0, rows):
                even[pl.ds(base + b * 8, 16)] = high
                even_low[pl.ds(base + b * 8, 16)] = low
        else:
            for base in (0, rows):
                odd[pl.ds(base + (b - 1) * 8, 16)] = high
                odd_low[pl.ds(base + (b - 1) * 8, 16)] = low
    total = jnp.zeros((rows, 2 * blk), F32)
    small = jnp.zeros((rows, blk), F32)
    for k in range(0, det, 2):
        first = pl.ds((det - k) * 8 % rows, rows)
        second = pl.ds((det - k - 2) * 8, rows)
        weight = ramp_ref[pl.ds(k * blk, 2 * blk)]
        high = jnp.concatenate([even[first], odd[second]], axis=1)
        low = jnp.concatenate([even_low[first], odd_low[second]], axis=1)
        total = total + lax.dot_general(high, weight, CONTRACT_INNER, preferred_element_type=F32)
        small = small + lax.dot_general(low, weight[:, :blk], CONTRACT_INNER, preferred_element_type=F32)
    small = small + total[:, blk:] + total[:, :blk]
    for b in range(0, det, 2):
        pair = jnp.concatenate([new_ref[:, pl.ds(b * blk, blk)], new_ref[:, pl.ds((b + 1) * blk, blk)]], axis=0)
        q_ref[me, pl.ds(b * 8, 16)] = (0.5 * pair + small[b * 8 : b * 8 + 16]).astype(BF16)

    halves = 2
    step = rows // halves
    across, around, onward = [], [], []
    for c in range(halves):
        mine = q_ref.at[me, pl.ds(c * step, step)]
        copy = remote(mine, mine, gz_s.at[c], gz_r.at[c], partner)
        copy.start()
        across.append(copy)
    for d, t in enumerate(peers):
        copy = remote(q_ref.at[me], q_ref.at[me], gx_s.at[d], gx_r.at[d], (slab, 2 * t + z))
        copy.start()
        around.append(copy)
    for c in range(halves):
        across[c].wait_recv()
        theirs = q_ref.at[2 * x + 1 - z, pl.ds(c * step, step)]
        for d, t in enumerate(peers):
            copy = remote(theirs, theirs, fx_s.at[d, c], fx_r.at[d, c], (slab, 2 * t + z))
            copy.start()
            onward.append(copy)
    for copy in around + onward:
        copy.wait_recv()
    for line in x_copies:
        for copy in line:
            copy.wait_send()
    for copy in z_copies + across + around + onward:
        copy.wait_send()

    @pl.when(has_next)
    def _():
        to_next.wait_send()

    @pl.when(has_prev)
    def _():
        to_prev.wait_send()


def primal_kernel_body(
    slabs, vol_ref, back_ref, weights, new_ref, down, up, from_prev, from_next, send, recv
):
    slab, me = lax.axis_index("slab"), lax.axis_index("angle")
    has_prev, has_next = slab > 0, slab < slabs - 1
    prev, following = (slab - 1, me), (slab + 1, me)
    greet([], [(has_prev, prev), (has_next, following)])
    down[...] = weights[0, 0] * vol_ref[:, 7, :] + weights[1, 0] * back_ref[:, 7, :]
    up[...] = weights[0, 2] * vol_ref[:, 0, :] + weights[1, 2] * back_ref[:, 0, :]
    to_next = remote(down, from_prev, send.at[0], recv.at[0], following)
    to_prev = remote(up, from_next, send.at[1], recv.at[1], prev)

    @pl.when(has_next)
    def _():
        to_next.start()

    @pl.when(has_prev)
    def _():
        to_prev.start()

    row = lax.broadcasted_iota(jnp.int32, (1, 8, vol_ref.shape[2]), 1)

    def one(i, _):
        here = pl.ds(i * 8, 8)
        vol, back = vol_ref[here], back_ref[here]
        before = pltpu.roll(weights[0, 0] * vol + weights[1, 0] * back, 1, 1)
        after = pltpu.roll(weights[0, 2] * vol + weights[1, 2] * back, 7, 1)
        before = jnp.where(row == 0, 0.0, before)
        after = jnp.where(row == 7, 0.0, after)
        new_ref[here] = vol + weights[0, 1] * vol + weights[1, 1] * back + before + after
        return 0

    lax.fori_loop(0, vol_ref.shape[0] // 8, one, 0)

    @pl.when(has_prev)
    def _():
        to_next.wait_recv()
        new_ref[:, 0, :] += from_prev[...]

    @pl.when(has_next)
    def _():
        to_prev.wait_recv()
        new_ref[:, 7, :] += from_next[...]

    @pl.when(has_next)
    def _():
        to_next.wait_send()

    @pl.when(has_prev)
    def _():
        to_prev.wait_send()


def on_device(volume, dual, measured, tiles, lists, live, dual_kernel, primal_kernel):
    groups, slabs = lax.axis_size("angle"), lax.axis_size("slab")
    seg = lists.shape[2] // groups
    blocks, _, blk = volume.shape
    width = dual.shape[2]
    det = width // blk
    rows = det * 8
    vmem, smem = pl.BlockSpec(memory_space=pltpu.VMEM), pl.BlockSpec(memory_space=pltpu.SMEM)
    dma = pltpu.SemaphoreType.DMA

    parts = lists[:, 0].reshape(3, groups, seg)
    alive = jnp.arange(seg, dtype=jnp.int32)[None, :] < live[0][:, None]
    vox = parts[0] - jnp.arange(groups, dtype=jnp.int32)[:, None] * blocks
    rows_of = jnp.stack([vox, jnp.where(alive, parts[1], det), parts[2]], axis=1)
    rows_of = jnp.pad(rows_of, ((0, 0), (0, 5), (0, 0)))
    index = pl.pallas_call(
        functools.partial(lists_kernel, groups),
        out_shape=jax.ShapeDtypeStruct(rows_of.shape, jnp.int32),
        in_specs=[vmem],
        out_specs=vmem,
        scratch_shapes=[pltpu.VMEM(rows_of.shape, jnp.int32), dma((groups - 1,)), dma((groups - 1,))],
        compiler_params=pltpu.CompilerParams(collective_id=0, has_side_effects=True),
    )(rows_of)

    partial = pl.pallas_call(
        forward_kernel,
        out_shape=jax.ShapeDtypeStruct((groups, rows, blk), BF16),
        in_specs=[smem, vmem, vmem],
        out_specs=vmem,
        scratch_shapes=[
            pltpu.VMEM((tiles.shape[0] * blocks, 8, blk), F32),
            pltpu.VMEM((blocks * 8, blk), BF16),
        ]
        + [pltpu.VMEM((det + 1, 8, blk), F32)] * groups,
        compiler_params=pltpu.CompilerParams(vmem_limit_bytes=VMEM_LIMIT),
    )(index, volume, tiles)

    new_dual, filtered = pl.pallas_call(
        functools.partial(dual_kernel_body, slabs),
        out_shape=[
            jax.ShapeDtypeStruct((8, width), F32),
            jax.ShapeDtypeStruct((groups, rows, blk), BF16),
        ],
        in_specs=[vmem, vmem, vmem, vmem, smem],
        out_specs=[vmem, vmem],
        scratch_shapes=[
            pltpu.VMEM((X_SIZE - 1, 2, rows, blk), BF16),
            pltpu.VMEM((rows, blk), BF16),
            pltpu.VMEM((rows, blk), BF16),
            pltpu.VMEM((rows, blk), F32),
            pltpu.VMEM((8, width), F32),
        ]
        + [pltpu.VMEM((1, width), F32)] * 4
        + [pltpu.VMEM((2 * rows, blk), BF16)] * 4
        + [dma((X_SIZE - 1, CHUNKS))] * 2
        + [dma((CHUNKS,))] * 2
        + [dma((2,))] * 2
        + [dma((X_SIZE - 1,))] * 2
        + [dma((2,))] * 2
        + [dma((X_SIZE - 1, 2))] * 2,
        compiler_params=pltpu.CompilerParams(
            collective_id=1, has_side_effects=True, vmem_limit_bytes=VMEM_LIMIT
        ),
    )(partial, dual[0], measured[0], jnp.asarray(ramp_matrix(width, blk)), dual_kernel)

    back = pl.pallas_call(
        backward_kernel,
        out_shape=jax.ShapeDtypeStruct((blocks, 8, blk), F32),
        in_specs=[smem, vmem, vmem],
        out_specs=vmem,
        scratch_shapes=[
            pltpu.VMEM((groups * (det + 1), 8, blk), F32),
            pltpu.VMEM((tiles.shape[0] * blocks, 8, blk), F32),
        ],
        compiler_params=pltpu.CompilerParams(vmem_limit_bytes=VMEM_LIMIT),
    )(index, filtered, tiles)

    new_volume = pl.pallas_call(
        functools.partial(primal_kernel_body, slabs),
        out_shape=jax.ShapeDtypeStruct(volume.shape, F32),
        in_specs=[vmem, vmem, smem],
        out_specs=vmem,
        scratch_shapes=[pltpu.VMEM((blocks, blk), F32)] * 4 + [dma((2,))] * 2,
        compiler_params=pltpu.CompilerParams(
            collective_id=2, has_side_effects=True, vmem_limit_bytes=VMEM_LIMIT
        ),
    )(volume, back, primal_kernel)
    return (new_volume, new_dual[None])


def solution(mesh):
    in_specs = (
        P("angle", "slab", None),
        P("angle", "slab", None),
        P("angle", "slab", None),
        P(),
        P(None, "slab", "angle"),
        P("slab", "angle"),
        P(),
        P(),
    )
    out_specs = (P("angle", "slab", None), P("angle", "slab", None))
    return jax.shard_map(
        on_device, mesh=mesh, in_specs=in_specs, out_specs=out_specs, check_vma=False
    )
```

```python
import functools

import jax
import jax.numpy as jnp
import ml_dtypes
import numpy as np
from jax import lax
from jax.experimental import pallas as pl
from jax.experimental.pallas import tpu as pltpu
from jax.sharding import PartitionSpec as P

F32 = jnp.float32
BF16 = jnp.bfloat16
MESH = pl.DeviceIdType.MESH
CONTRACT_LAST = (((1,), (1,)), ((), ()))
CONTRACT_INNER = (((1,), (0,)), ((), ()))
VMEM_LIMIT = 56 * 2**20
X_SIZE = 4


def ramp_matrix(width, blk):
    n = np.arange(width)
    taps = np.zeros(width)
    odd = n % 2 == 1
    taps[odd] = -(2.0 / width**2) / np.sin(np.pi * n[odd] / width) ** 2
    k = np.arange(width // blk)[:, None, None]
    i = np.arange(blk)[None, :, None]
    j = np.arange(blk)[None, None, :]
    full = taps[(blk * k + j - i) % width].reshape(width, blk)
    high = full.astype(ml_dtypes.bfloat16)
    low = (full - high.astype(np.float64)).astype(ml_dtypes.bfloat16)
    return np.concatenate([high, low], axis=1)


def remote(src, dst, send, recv, device):
    return pltpu.make_async_remote_copy(
        src_ref=src, dst_ref=dst, send_sem=send, recv_sem=recv, device_id=device, device_id_type=MESH
    )


def step_kernel(
    slabs,
    lists_ref,
    live_ref,
    vol_ref,
    dual_ref,
    meas_ref,
    tiles_hbm,
    ramp_hbm,
    dual_w,
    primal_w,
    new_vol,
    new_dual,
    tiles,
    ramp,
    dense,
    rounded,
    out_lists,
    in_lists,
    index,
    picked,
    part,
    land_near,
    land_far,
    near,
    send_z,
    land_z,
    misfit,
    down,
    up,
    from_prev,
    from_next,
    far_prev,
    far_next,
    even,
    odd,
    even_low,
    odd_low,
    q_near,
    q_far,
    wide,
    terms,
    back,
    vol_down,
    vol_up,
    back_prev,
    back_next,
    load_sem,
    ls,
    lr,
    index_sem,
    ns,
    nr,
    fs,
    fr,
    zs,
    zr,
    es,
    er,
    ps,
    pr,
    gs,
    gr,
    hs,
    hr,
    ws,
    wr,
    vs,
    vr,
):
    slab, me = lax.axis_index("slab"), lax.axis_index("angle")
    x, z = me // 2, lax.rem(me, 2)
    has_prev, has_next = slab > 0, slab < slabs - 1
    blocks, _, blk = vol_ref.shape
    width = dual_ref.shape[1]
    det = width // blk
    rows = det * 8
    seg = blk
    pairs = 8 * seg
    tile_count = tiles.shape[0]

    def group(k):
        return 2 * lax.rem(x + k % 4, 4) + (1 - z if k >= 4 else z)

    def device(k):
        return (slab, group(k))

    def mirror(k):
        return (4 - k % 4) % 4 + 4 * (k // 4)

    prev, following = (slab - 1, me), (slab + 1, me)
    far_me = 2 * x + 1 - z
    prev_far, following_far = (slab - 1, far_me), (slab + 1, far_me)

    barrier = pltpu.get_barrier_semaphore()
    for k in range(1, 8):
        pl.semaphore_signal(barrier, inc=1, device_id=device(k), device_id_type=MESH)

    @pl.when(has_prev)
    def _():
        pl.semaphore_signal(barrier, inc=1, device_id=prev, device_id_type=MESH)
        pl.semaphore_signal(barrier, inc=1, device_id=prev_far, device_id_type=MESH)

    @pl.when(has_next)
    def _():
        pl.semaphore_signal(barrier, inc=1, device_id=following, device_id_type=MESH)
        pl.semaphore_signal(barrier, inc=1, device_id=following_far, device_id_type=MESH)

    load_tiles = pltpu.make_async_copy(tiles_hbm, tiles, load_sem.at[0])
    load_ramp = pltpu.make_async_copy(ramp_hbm, ramp, load_sem.at[1])
    load_tiles.start()
    load_ramp.start()

    lane = lax.broadcasted_iota(jnp.int32, (1, seg), 1)
    for j in range(8):
        cols = pl.ds(j * seg, seg)
        out_lists[j, 0:1, :] = jnp.clip(lists_ref[0, :, cols] - j * blocks, 0, blocks - 1)
        out_lists[j, 1:2, :] = jnp.where(lane < live_ref[0, j], lists_ref[1, :, cols], det)
        out_lists[j, 2:3, :] = lists_ref[2, :, cols]
        out_lists[j, 3:8, :] = jnp.zeros((5, seg), jnp.int32)

    rounded[...] = vol_ref[...].reshape(blocks * 8, blk).astype(BF16)
    vol_down[...] = vol_ref[:, 7, :] * primal_w[0, 0]
    vol_up[...] = vol_ref[:, 0, :] * primal_w[0, 2]
    for k in range(8):
        wide[k * (det + 1) + det] = jnp.zeros((8, blk), F32)
    load_tiles.wait()

    def products(i, _):
        for u in range(0, 8, 2):
            t = i * 8 + u
            both = lax.dot_general(
                rounded[...], tiles[pl.ds(t, 2)].reshape(2 * blk, blk), CONTRACT_LAST, preferred_element_type=F32
            )
            dense[pl.ds(t * blocks, blocks)] = both[:, :blk].reshape(blocks, 8, blk)
            dense[pl.ds((t + 1) * blocks, blocks)] = both[:, blk:].reshape(blocks, 8, blk)
        return 0

    half = tile_count // 16
    lax.fori_loop(0, half, products, 0)
    present = 2 * (has_prev.astype(jnp.int32) + has_next.astype(jnp.int32))
    pl.semaphore_wait(barrier, 7 + present)

    list_copies = {}
    for k in (4, 6, 5, 7, 2, 1, 3):
        list_copies[k] = remote(
            out_lists.at[group(k)], in_lists.at[mirror(k)], ls.at[k - 1], lr.at[mirror(k) - 1], device(k)
        )
        list_copies[k].start()
    in_lists[0] = out_lists[me]
    lax.fori_loop(half, 2 * half, products, 0)

    row = lax.broadcasted_iota(jnp.int32, (1, 8, blk), 1)

    def volume_part(i, _):
        here = pl.ds(i * 8, 8)
        vol = vol_ref[here]
        before = jnp.where(row == 0, 0.0, pltpu.roll(primal_w[0, 0] * vol, 1, 1))
        after = jnp.where(row == 7, 0.0, pltpu.roll(primal_w[0, 2] * vol, 7, 1))
        new_vol[here] = vol + primal_w[0, 1] * vol + before + after
        return 0

    lax.fori_loop(0, blocks // 8, volume_part, 0)

    def split(value):
        high = value.astype(BF16)
        return high, (value - high.astype(F32)).astype(BF16)

    def to_index(k):
        copy = pltpu.make_async_copy(in_lists.at[k], index.at[k], index_sem.at[k])
        copy.start()
        return copy

    det_row = lax.broadcasted_iota(jnp.int32, (det, seg), 0)

    def project(k):
        def pick(j, _):
            for u in range(16):
                i = j * 16 + u
                picked[pl.ds(i, 8, stride=seg), :] = dense[index[k, 2, i] * blocks + index[k, 0, i]]
            return 0

        lax.fori_loop(0, seg // 16, pick, 0)
        parts = [split(picked[pl.ds(r * seg, seg)]) for r in range(8)]
        stacked = jnp.concatenate(
            [jnp.concatenate([p[0] for p in parts], axis=1), jnp.concatenate([p[1] for p in parts], axis=1)], axis=0
        )
        hot = jnp.where(det_row == in_lists[k, 1:2, :], 1.0, 0.0).astype(BF16)
        summed = jnp.dot(jnp.concatenate([hot, hot], axis=1), stacked, preferred_element_type=F32)
        for r in range(8):
            here = pl.ds(r * det, det)
            value = summed[:, r * blk : (r + 1) * blk]
            if k == 0:
                near[here] = value
            else:
                part[k - 1, here] = value.astype(BF16)

    near_copies, far_copies = [], []

    def send_part(k):
        d = k % 4
        if k < 4:
            copy = remote(part.at[k - 1], land_near.at[mirror(k) - 1], ns.at[d - 1], nr.at[mirror(d) - 1], device(d))
            near_copies.append(copy)
        else:
            copy = remote(part.at[k - 1], land_far.at[mirror(d) - 1], fs.at[d - 1], fr.at[mirror(d) - 1], device(d))
            far_copies.append(copy)
        copy.start()

    for k in (1, 3, 2):
        list_copies[k].wait_recv()
    moves = [to_index(k) for k in (0, 1, 3, 2)]
    for move in moves:
        move.wait()
    for k in (1, 3, 2):
        project(k)
        send_part(k)
    project(0)
    for k in (4, 5, 7, 6):
        list_copies[k].wait_recv()
    moves = [to_index(k) for k in (4, 5, 7, 6)]
    for move in moves:
        move.wait()
    for k in (6, 5, 7):
        project(k)
        send_part(k)
    project(4)

    for copy in far_copies:
        copy.wait_recv()
    total = part[3].astype(F32)
    for d in range(3):
        total = total + land_far[d].astype(F32)
    send_z[...] = total.astype(BF16)
    across = remote(send_z, land_z, zs.at[0], zr.at[0], device(4))
    across.start()
    first, last = pl.ds(0, det), pl.ds(rows - det, det)
    far_up = remote(send_z.at[first], far_next, ps.at[0], pr.at[0], prev_far)
    far_down = remote(send_z.at[last], far_prev, ps.at[1], pr.at[1], following_far)

    @pl.when(has_prev)
    def _():
        far_up.start()

    @pl.when(has_next)
    def _():
        far_down.start()

    for copy in near_copies:
        copy.wait_recv()
    whole = pl.ds(0, rows)
    total = near[whole]
    for d in range(3):
        total = total + land_near[d].astype(F32)
    near[whole] = total
    for b in range(det):
        cols = pl.ds(b * blk, blk)
        misfit[:, cols] = near[pl.ds(b, 8, stride=det), :] - meas_ref[:, cols]
    down[...] = dual_w[0, 0] * dual_ref[7:8, :] + dual_w[1, 0] * misfit[7:8, :]
    up[...] = dual_w[0, 2] * dual_ref[0:1, :] + dual_w[1, 2] * misfit[0:1, :]
    near_down = remote(down, from_prev, es.at[0], er.at[0], following)
    near_up = remote(up, from_next, es.at[1], er.at[1], prev)

    @pl.when(has_next)
    def _():
        near_down.start()

    @pl.when(has_prev)
    def _():
        near_up.start()

    @pl.when(has_prev)
    def _():
        near_down.wait_recv()
        far_down.wait_recv()

    @pl.when(jnp.logical_not(has_prev))
    def _():
        from_prev[...] = jnp.zeros_like(from_prev)
        far_prev[...] = jnp.zeros_like(far_prev)

    @pl.when(has_next)
    def _():
        near_up.wait_recv()
        far_up.wait_recv()

    @pl.when(jnp.logical_not(has_next))
    def _():
        from_next[...] = jnp.zeros_like(from_next)
        far_next[...] = jnp.zeros_like(far_next)

    load_ramp.wait()
    across.wait_recv()
    near[whole] = land_z[...].astype(F32)
    flat_row = lax.broadcasted_iota(jnp.int32, (8, blk), 0)
    before_far = far_prev[...].astype(F32) * dual_w[1, 0]
    after_far = far_next[...].astype(F32) * dual_w[1, 2]

    def updated(b):
        cols = pl.ds(b * blk, blk)
        dual = dual_ref[:, cols]
        mis = misfit[:, cols] + near[pl.ds(b, 8, stride=det), :]
        before = pltpu.roll(dual_w[0, 0] * dual + dual_w[1, 0] * mis, 1, 0)
        after = pltpu.roll(dual_w[0, 2] * dual + dual_w[1, 2] * mis, 7, 0)
        before = jnp.where(flat_row == 0, from_prev[:, cols] + before_far[b : b + 1], before)
        after = jnp.where(flat_row == 7, from_next[:, cols] + after_far[b : b + 1], after)
        new = dual + dual_w[0, 1] * dual + dual_w[1, 1] * mis + before + after
        new_dual[:, cols] = new
        return new

    news = [updated(b) for b in range(det)]
    for b in range(det):
        high, low = split(jnp.concatenate([news[b], news[(b + 1) % det]], axis=0))
        for base in (0, rows):
            if b % 2 == 0:
                even[pl.ds(base + b * 8, 16)] = high
                even_low[pl.ds(base + b * 8, 16)] = low
            else:
                odd[pl.ds(base + (b - 1) * 8, 16)] = high
                odd_low[pl.ds(base + (b - 1) * 8, 16)] = low
    total = jnp.zeros((rows, 2 * blk), F32)
    small = jnp.zeros((rows, blk), F32)
    for k in range(0, det, 2):
        here = pl.ds((det - k) * 8 % rows, rows)
        there = pl.ds((det - k - 2) * 8, rows)
        weight = ramp[pl.ds(k * blk, 2 * blk)]
        high = jnp.concatenate([even[here], odd[there]], axis=1)
        low = jnp.concatenate([even_low[here], odd_low[there]], axis=1)
        total = total + jnp.dot(high, weight, preferred_element_type=F32)
        small = small + jnp.dot(low, weight[:, :blk], preferred_element_type=F32)
    small = small + total[:, blk:] + total[:, :blk]
    for b in range(0, det, 2):
        both = jnp.concatenate([new_dual[:, pl.ds(b * blk, blk)], new_dual[:, pl.ds((b + 1) * blk, blk)]], axis=0)
        q_near[0, pl.ds(b * 8, 16)] = (0.5 * both + small[b * 8 : b * 8 + 16]).astype(BF16)

    over = remote(q_near.at[0], q_far.at[0], gs.at[0], gr.at[0], device(4))
    over.start()
    around = []
    for k in (2, 1, 3):
        copy = remote(q_near.at[0], q_near.at[mirror(k)], hs.at[k - 1], hr.at[mirror(k) - 1], device(k))
        copy.start()
        around.append(copy)

    def widen(k, value):
        wide[pl.ds(k * (det + 1), det)] = value.reshape(det, 8, blk).astype(F32)

    none = jnp.zeros((8, blk), F32)

    def back_products(lo, hi):
        def some(j, _):
            k = j // 2
            for u in range(0, 64, 2):
                sides = []
                for w in range(2):
                    i = lax.rem(j, 2) * 64 + u + w
                    value = wide[k * (det + 1) + index[k, 1, i]]
                    sides.append(jnp.concatenate([value, none] if w == 0 else [none, value], axis=0))
                i = lax.rem(j, 2) * 64 + u
                weight = jnp.concatenate([tiles[index[k, 2, i]], tiles[index[k, 2, i + 1]]], axis=0)
                left = jnp.concatenate(sides, axis=1).astype(BF16)
                both = jnp.dot(left, weight, preferred_element_type=F32)
                p = k * seg + i
                terms[pl.ds(p, 8, stride=pairs), :] = both[:8]
                terms[pl.ds(p + 1, 8, stride=pairs), :] = both[8:]
            return 0

        lax.fori_loop(2 * lo, 2 * hi, some, 0)

    vox_row = lax.broadcasted_iota(jnp.int32, (blocks, seg), 0)

    def hots(lo):
        hot = [jnp.where(vox_row == in_lists[k, 0:1, :], 1.0, 0.0).astype(BF16) for k in range(lo, lo + 4)]
        return jnp.concatenate(hot + hot, axis=1)

    def scattered(hot, lo, r):
        high, low = split(terms[pl.ds(r * pairs + lo * seg, 4 * seg)])
        return jnp.dot(hot, jnp.concatenate([high, low], axis=0), preferred_element_type=F32)

    widen(0, q_near[0])
    back_products(0, 1)
    for copy in around:
        copy.wait_recv()
    for k in range(1, 4):
        widen(k, q_near[k])
    back_products(1, 4)
    hot = hots(0)
    for r in range(8):
        back[pl.ds(r * blocks, blocks)] = scattered(hot, 0, r)

    over.wait_recv()
    onward = []
    for k in (2, 1, 3):
        copy = remote(q_far.at[0], q_far.at[mirror(k)], ws.at[k - 1], wr.at[mirror(k) - 1], device(k))
        copy.start()
        onward.append(copy)
    widen(4, q_far[0])
    back_products(4, 5)
    for copy in onward:
        copy.wait_recv()
    for k in range(1, 4):
        widen(4 + k, q_far[k])
    back_products(5, 8)
    hot = hots(4)

    def finish(r):
        back[pl.ds(r * blocks, blocks)] += scattered(hot, 4, r)

    finish(0)
    finish(7)
    vol_up[...] += primal_w[1, 2] * back[pl.ds(0, blocks)]
    vol_down[...] += primal_w[1, 0] * back[pl.ds(7 * blocks, blocks)]
    to_next = remote(vol_down, back_prev, vs.at[0], vr.at[0], following)
    to_prev = remote(vol_up, back_next, vs.at[1], vr.at[1], prev)

    @pl.when(has_next)
    def _():
        to_next.start()

    @pl.when(has_prev)
    def _():
        to_prev.start()

    for r in range(1, 7):
        finish(r)

    for r in range(8):
        value = primal_w[1, 1] * back[pl.ds(r * blocks, blocks)]
        if r > 0:
            value = value + primal_w[1, 0] * back[pl.ds((r - 1) * blocks, blocks)]
        if r < 7:
            value = value + primal_w[1, 2] * back[pl.ds((r + 1) * blocks, blocks)]
        terms[pl.ds(r * blocks, blocks)] = value

    @pl.when(has_prev)
    def _():
        to_next.wait_recv()
        terms[pl.ds(0, blocks)] += back_prev[...]

    @pl.when(has_next)
    def _():
        to_prev.wait_recv()
        terms[pl.ds(7 * blocks, blocks)] += back_next[...]

    def merge(i, _):
        for u in range(16):
            v = i * 16 + u
            new_vol[v] += terms[pl.ds(v, 8, stride=blocks), :]
        return 0

    lax.fori_loop(0, blocks // 16, merge, 0)

    for copy in list(list_copies.values()) + near_copies + far_copies + [across, over] + around + onward:
        copy.wait_send()

    @pl.when(has_prev)
    def _():
        far_up.wait_send()
        near_up.wait_send()
        to_prev.wait_send()

    @pl.when(has_next)
    def _():
        far_down.wait_send()
        near_down.wait_send()
        to_next.wait_send()


def on_device(volume, dual, measured, tiles, lists, live, dual_kernel, primal_kernel):
    groups, slabs = lax.axis_size("angle"), lax.axis_size("slab")
    blocks, _, blk = volume.shape
    width = dual.shape[2]
    det = width // blk
    rows = det * 8
    vmem, smem = pl.BlockSpec(memory_space=pltpu.VMEM), pl.BlockSpec(memory_space=pltpu.SMEM)
    hbm = pl.BlockSpec(memory_space=pl.ANY)
    dma = pltpu.SemaphoreType.DMA
    ramp = jnp.asarray(ramp_matrix(width, blk))
    new_volume, new_dual = pl.pallas_call(
        functools.partial(step_kernel, slabs),
        out_shape=[jax.ShapeDtypeStruct(volume.shape, F32), jax.ShapeDtypeStruct((8, width), F32)],
        in_specs=[vmem, smem, vmem, vmem, vmem, hbm, hbm, smem, smem],
        out_specs=[vmem, vmem],
        scratch_shapes=[
            pltpu.VMEM(tiles.shape, BF16),
            pltpu.VMEM(ramp.shape, BF16),
            pltpu.VMEM((tiles.shape[0] * blocks, 8, blk), F32),
            pltpu.VMEM((blocks * 8, blk), BF16),
            pltpu.VMEM((groups, 8, blk), jnp.int32),
            pltpu.VMEM((groups, 8, blk), jnp.int32),
            pltpu.SMEM((groups, 8, blk), jnp.int32),
            pltpu.VMEM((9 * blk, blk), F32),
            pltpu.VMEM((7, rows, blk), BF16),
            pltpu.VMEM((3, rows, blk), BF16),
            pltpu.VMEM((3, rows, blk), BF16),
            pltpu.VMEM((rows + det, blk), F32),
            pltpu.VMEM((rows, blk), BF16),
            pltpu.VMEM((rows, blk), BF16),
            pltpu.VMEM((8, width), F32),
        ]
        + [pltpu.VMEM((1, width), F32)] * 4
        + [pltpu.VMEM((det, blk), BF16)] * 2
        + [pltpu.VMEM((2 * rows, blk), BF16)] * 4
        + [pltpu.VMEM((4, rows, blk), BF16)] * 2
        + [
            pltpu.VMEM((groups * (det + 1), 8, blk), F32),
            pltpu.VMEM((9 * groups * blk, blk), F32),
            pltpu.VMEM((8 * blocks, blk), F32),
        ]
        + [pltpu.VMEM((blocks, blk), F32)] * 4
        + [dma((2,)), dma((7,)), dma((7,)), dma((8,))]
        + [dma((3,))] * 4
        + [dma((1,))] * 2
        + [dma((2,))] * 4
        + [dma((1,))] * 2
        + [dma((3,))] * 4
        + [dma((2,))] * 2,
        compiler_params=pltpu.CompilerParams(
            collective_id=0, has_side_effects=True, vmem_limit_bytes=VMEM_LIMIT
        ),
    )(lists, live, volume, dual[0], measured[0], tiles, ramp, dual_kernel, primal_kernel)
    return (new_volume, new_dual[None])


def solution(mesh):
    in_specs = (
        P("angle", "slab", None),
        P("angle", "slab", None),
        P("angle", "slab", None),
        P(),
        P(None, "slab", "angle"),
        P("slab", "angle"),
        P(),
        P(),
    )
    out_specs = (P("angle", "slab", None), P("angle", "slab", None))
    return jax.shard_map(
        on_device, mesh=mesh, in_specs=in_specs, out_specs=out_specs, check_vma=False
    )
```

```python
import functools

import jax
import jax.numpy as jnp
import ml_dtypes
import numpy as np
from jax import lax
from jax.experimental import pallas as pl
from jax.experimental.pallas import tpu as pltpu
from jax.sharding import PartitionSpec as P

F32 = jnp.float32
BF16 = jnp.bfloat16
MESH = pl.DeviceIdType.MESH
CONTRACT_LAST = (((1,), (1,)), ((), ()))
CONTRACT_INNER = (((1,), (0,)), ((), ()))
VMEM_LIMIT = 56 * 2**20
X_SIZE = 4


def ramp_matrix(width, blk):
    n = np.arange(width)
    taps = np.zeros(width)
    odd = n % 2 == 1
    taps[odd] = -(2.0 / width**2) / np.sin(np.pi * n[odd] / width) ** 2
    k = np.arange(width // blk)[:, None, None]
    i = np.arange(blk)[None, :, None]
    j = np.arange(blk)[None, None, :]
    full = taps[(blk * k + j - i) % width].reshape(width, blk)
    high = full.astype(ml_dtypes.bfloat16)
    low = (full - high.astype(np.float64)).astype(ml_dtypes.bfloat16)
    return np.concatenate([high, low], axis=1)


def remote(src, dst, send, recv, device):
    return pltpu.make_async_remote_copy(
        src_ref=src, dst_ref=dst, send_sem=send, recv_sem=recv, device_id=device, device_id_type=MESH
    )


def step_kernel(
    slabs,
    lists_ref,
    live_ref,
    vol_hbm,
    dual_hbm,
    meas_hbm,
    tiles_hbm,
    ramp_hbm,
    dual_w,
    primal_w,
    new_vol,
    new_dual,
    vol_ref,
    dual_ref,
    meas_ref,
    tiles,
    ramp,
    dense,
    rounded,
    out_lists,
    in_lists,
    prepared,
    index,
    picked,
    part,
    land_near,
    land_far,
    near,
    send_z,
    land_z,
    misfit,
    down,
    up,
    from_prev,
    from_next,
    far_prev,
    far_next,
    even,
    odd,
    even_low,
    odd_low,
    q_near,
    q_far,
    wide,
    terms,
    back,
    vol_down,
    vol_up,
    back_prev,
    back_next,
    load_sem,
    ls,
    lr,
    index_sem,
    ns,
    nr,
    fs,
    fr,
    zs,
    zr,
    es,
    er,
    ps,
    pr,
    gs,
    gr,
    hs,
    hr,
    ws,
    wr,
    vs,
    vr,
):
    slab, me = lax.axis_index("slab"), lax.axis_index("angle")
    x, z = me // 2, lax.rem(me, 2)
    has_prev, has_next = slab > 0, slab < slabs - 1
    blocks, _, blk = vol_ref.shape
    width = dual_ref.shape[1]
    det = width // blk
    rows = det * 8
    seg = blk
    pairs = 8 * seg
    tile_count = tiles.shape[0]

    def group(k):
        return 2 * lax.rem(x + k % 4, 4) + (1 - z if k >= 4 else z)

    def device(k):
        return (slab, group(k))

    def mirror(k):
        return (4 - k % 4) % 4 + 4 * (k // 4)

    prev, following = (slab - 1, me), (slab + 1, me)
    far_me = 2 * x + 1 - z
    prev_far, following_far = (slab - 1, far_me), (slab + 1, far_me)

    barrier = pltpu.get_barrier_semaphore()
    for k in range(1, 8):
        pl.semaphore_signal(barrier, inc=1, device_id=device(k), device_id_type=MESH)

    @pl.when(has_prev)
    def _():
        pl.semaphore_signal(barrier, inc=1, device_id=prev, device_id_type=MESH)
        pl.semaphore_signal(barrier, inc=1, device_id=prev_far, device_id_type=MESH)

    @pl.when(has_next)
    def _():
        pl.semaphore_signal(barrier, inc=1, device_id=following, device_id_type=MESH)
        pl.semaphore_signal(barrier, inc=1, device_id=following_far, device_id_type=MESH)

    loads = [
        pltpu.make_async_copy(source, target, load_sem.at[i])
        for i, (source, target) in enumerate(
            [(tiles_hbm, tiles), (vol_hbm, vol_ref), (dual_hbm, dual_ref), (meas_hbm, meas_ref), (ramp_hbm, ramp)]
        )
    ]
    for load in loads:
        load.start()

    lane = lax.broadcasted_iota(jnp.int32, (1, seg), 1)
    for j in range(8):
        cols = pl.ds(j * seg, seg)
        out_lists[j, 0:1, :] = jnp.clip(lists_ref[0, :, cols] - j * blocks, 0, blocks - 1)
        out_lists[j, 1:2, :] = jnp.where(lane < live_ref[0, j], lists_ref[1, :, cols], det)
        out_lists[j, 2:3, :] = lists_ref[2, :, cols]
        out_lists[j, 3:8, :] = jnp.zeros((5, seg), jnp.int32)

    def prepare(k):
        voxel, detector, tile = in_lists[k, 0:1, :], in_lists[k, 1:2, :], in_lists[k, 2:3, :]
        prepared[k, 0:1, :] = tile * blocks + voxel
        prepared[k, 1:2, :] = detector + k * (det + 1)
        prepared[k, 2:8, :] = in_lists[k, 2:8, :]
        copy = pltpu.make_async_copy(prepared.at[k], index.at[k], index_sem.at[k])
        copy.start()
        return copy

    in_lists[0] = out_lists[me]
    own_index = prepare(0)
    loads[0].wait()
    loads[1].wait()
    rounded[...] = vol_ref[...].reshape(blocks * 8, blk).astype(BF16)

    def products(i, _):
        for u in range(0, 8, 2):
            t = i * 8 + u
            both = lax.dot_general(
                rounded[...], tiles[pl.ds(t, 2)].reshape(2 * blk, blk), CONTRACT_LAST, preferred_element_type=F32
            )
            dense[pl.ds(t * blocks, blocks)] = both[:, :blk].reshape(blocks, 8, blk)
            dense[pl.ds((t + 1) * blocks, blocks)] = both[:, blk:].reshape(blocks, 8, blk)
        return 0

    early = tile_count // 8 - 2
    lax.fori_loop(0, early, products, 0)
    present = 2 * (has_prev.astype(jnp.int32) + has_next.astype(jnp.int32))
    pl.semaphore_wait(barrier, 7 + present)

    list_copies = {}
    for k in (6, 5, 7, 4, 2, 1, 3):
        list_copies[k] = remote(
            out_lists.at[group(k)], in_lists.at[mirror(k)], ls.at[k - 1], lr.at[mirror(k) - 1], device(k)
        )
        list_copies[k].start()
    lax.fori_loop(early, tile_count // 8, products, 0)

    def split(value):
        high = value.astype(BF16)
        return high, (value - high.astype(F32)).astype(BF16)

    det_row = lax.broadcasted_iota(jnp.int32, (det, seg), 0)

    def project(k):
        def pick(j, _):
            for u in range(32):
                i = j * 32 + u
                picked[pl.ds(i, 8, stride=seg + 8), :] = dense[index[k, 0, i]]
            return 0

        lax.fori_loop(0, seg // 32, pick, 0)
        parts = [split(picked[pl.ds(r * (seg + 8), seg)]) for r in range(8)]
        stacked = jnp.concatenate(
            [jnp.concatenate([p[0] for p in parts], axis=1), jnp.concatenate([p[1] for p in parts], axis=1)], axis=0
        )
        hot = jnp.where(det_row == in_lists[k, 1:2, :], 1.0, 0.0).astype(BF16)
        return jnp.dot(jnp.concatenate([hot, hot], axis=1), stacked, preferred_element_type=F32)

    def turn(j):
        return lax.rem(j * (j + 1) // 2, 4)

    near_copies = {
        d: remote(part.at[d], land_near.at[mirror(d) - 1], ns.at[d - 1], nr.at[mirror(d) - 1], device(d))
        for d in (1, 3, 2)
    }
    far_copies = {
        d: remote(part.at[d + 4], land_far.at[mirror(d) - 1], fs.at[d - 1], fr.at[mirror(d) - 1], device(d))
        for d in (2, 3, 1)
    }

    def at_step(j, step):
        return pl.when(j == step)

    def receive(ks):
        for k in ks:
            list_copies[k].wait_recv()
        copies = [prepare(k) for k in ks]
        for copy in copies:
            copy.wait()

    def near_part(j, _):
        k = turn(j)

        @at_step(j, 1)
        def _():
            receive((1, 3, 2))

        summed = project(k)
        for r in range(8):
            here = pl.ds(r * det, det)
            part[k, here] = summed[:, r * blk : (r + 1) * blk].astype(BF16)

        @at_step(j, 0)
        def _():
            for r in range(8):
                near[pl.ds(r * det, det)] = summed[:, r * blk : (r + 1) * blk]

        for step, d in ((1, 1), (2, 3), (3, 2)):

            @at_step(j, step)
            def _():
                near_copies[d].start()

        return 0

    def far_part(j, _):
        k = 4 + turn(3 - j)
        summed = project(k)
        for r in range(8):
            here = pl.ds(r * det, det)
            part[k, here] = summed[:, r * blk : (r + 1) * blk].astype(BF16)

        for step, d in ((0, 2), (1, 3), (2, 1)):

            @at_step(j, step)
            def _():
                far_copies[d].start()

        return 0

    own_index.wait()
    lax.fori_loop(0, 4, near_part, 0)
    receive((4, 5, 7, 6))
    lax.fori_loop(0, 4, far_part, 0)

    for copy in far_copies.values():
        copy.wait_recv()
    total = part[4].astype(F32)
    for d in range(3):
        total = total + land_far[d].astype(F32)
    send_z[...] = total.astype(BF16)
    across = remote(send_z, land_z, zs.at[0], zr.at[0], device(4))
    across.start()
    first, last = pl.ds(0, det), pl.ds(rows - det, det)
    far_up = remote(send_z.at[first], far_next, ps.at[0], pr.at[0], prev_far)
    far_down = remote(send_z.at[last], far_prev, ps.at[1], pr.at[1], following_far)

    @pl.when(has_prev)
    def _():
        far_up.start()

    @pl.when(has_next)
    def _():
        far_down.start()

    loads[2].wait()
    loads[3].wait()
    for copy in near_copies.values():
        copy.wait_recv()
    whole = pl.ds(0, rows)
    total = near[whole]
    for d in range(3):
        total = total + land_near[d].astype(F32)
    near[whole] = total
    for b in range(det):
        cols = pl.ds(b * blk, blk)
        misfit[:, cols] = near[pl.ds(b, 8, stride=det), :] - meas_ref[:, cols]
    down[...] = dual_w[0, 0] * dual_ref[7:8, :] + dual_w[1, 0] * misfit[7:8, :]
    up[...] = dual_w[0, 2] * dual_ref[0:1, :] + dual_w[1, 2] * misfit[0:1, :]
    near_down = remote(down, from_prev, es.at[0], er.at[0], following)
    near_up = remote(up, from_next, es.at[1], er.at[1], prev)

    @pl.when(has_next)
    def _():
        near_down.start()

    @pl.when(has_prev)
    def _():
        near_up.start()

    vol_down[...] = vol_ref[:, 7, :] * primal_w[0, 0]
    vol_up[...] = vol_ref[:, 0, :] * primal_w[0, 2]
    for k in range(8):
        wide[k * (det + 1) + det] = jnp.zeros((8, blk), F32)
    row = lax.broadcasted_iota(jnp.int32, (1, 8, blk), 1)

    def volume_part(i, _):
        here = pl.ds(i * 8, 8)
        vol = vol_ref[here]
        before = jnp.where(row == 0, 0.0, pltpu.roll(primal_w[0, 0] * vol, 1, 1))
        after = jnp.where(row == 7, 0.0, pltpu.roll(primal_w[0, 2] * vol, 7, 1))
        new_vol[here] = vol + primal_w[0, 1] * vol + before + after
        return 0

    lax.fori_loop(0, blocks // 8, volume_part, 0)
    loads[4].wait()

    @pl.when(has_prev)
    def _():
        near_down.wait_recv()
        far_down.wait_recv()

    @pl.when(jnp.logical_not(has_prev))
    def _():
        from_prev[...] = jnp.zeros_like(from_prev)
        far_prev[...] = jnp.zeros_like(far_prev)

    @pl.when(has_next)
    def _():
        near_up.wait_recv()
        far_up.wait_recv()

    @pl.when(jnp.logical_not(has_next))
    def _():
        from_next[...] = jnp.zeros_like(from_next)
        far_next[...] = jnp.zeros_like(far_next)

    across.wait_recv()
    near[whole] = land_z[...].astype(F32)
    flat_row = lax.broadcasted_iota(jnp.int32, (8, blk), 0)
    before_far = far_prev[...].astype(F32) * dual_w[1, 0]
    after_far = far_next[...].astype(F32) * dual_w[1, 2]

    def updated(b):
        cols = pl.ds(b * blk, blk)
        dual = dual_ref[:, cols]
        mis = misfit[:, cols] + near[pl.ds(b, 8, stride=det), :]
        before = pltpu.roll(dual_w[0, 0] * dual + dual_w[1, 0] * mis, 1, 0)
        after = pltpu.roll(dual_w[0, 2] * dual + dual_w[1, 2] * mis, 7, 0)
        before = jnp.where(flat_row == 0, from_prev[:, cols] + before_far[b : b + 1], before)
        after = jnp.where(flat_row == 7, from_next[:, cols] + after_far[b : b + 1], after)
        new = dual + dual_w[0, 1] * dual + dual_w[1, 1] * mis + before + after
        new_dual[:, cols] = new
        return new

    news = [updated(b) for b in range(det)]
    for b in range(det):
        high, low = split(jnp.concatenate([news[b], news[(b + 1) % det]], axis=0))
        for base in (0, rows):
            if b % 2 == 0:
                even[pl.ds(base + b * 8, 16)] = high
                even_low[pl.ds(base + b * 8, 16)] = low
            else:
                odd[pl.ds(base + (b - 1) * 8, 16)] = high
                odd_low[pl.ds(base + (b - 1) * 8, 16)] = low
    total = jnp.zeros((rows, 2 * blk), F32)
    small = jnp.zeros((rows, blk), F32)
    for k in range(0, det, 2):
        here = pl.ds((det - k) * 8 % rows, rows)
        there = pl.ds((det - k - 2) * 8, rows)
        weight = ramp[pl.ds(k * blk, 2 * blk)]
        high = jnp.concatenate([even[here], odd[there]], axis=1)
        low = jnp.concatenate([even_low[here], odd_low[there]], axis=1)
        total = total + jnp.dot(high, weight, preferred_element_type=F32)
        small = small + jnp.dot(low, weight[:, :blk], preferred_element_type=F32)
    small = small + total[:, blk:] + total[:, :blk]
    for b in range(0, det, 2):
        both = jnp.concatenate([new_dual[:, pl.ds(b * blk, blk)], new_dual[:, pl.ds((b + 1) * blk, blk)]], axis=0)
        q_near[0, pl.ds(b * 8, 16)] = (0.5 * both + small[b * 8 : b * 8 + 16]).astype(BF16)

    over = remote(q_near.at[0], q_far.at[0], gs.at[0], gr.at[0], device(4))
    over.start()
    around, onward = {}, {}
    for k in (2, 1, 3):
        around[k] = remote(q_near.at[0], q_near.at[mirror(k)], hs.at[k - 1], hr.at[mirror(k) - 1], device(k))
        around[k].start()
        onward[k] = remote(q_far.at[0], q_far.at[mirror(k)], ws.at[k - 1], wr.at[mirror(k) - 1], device(k))

    def widen(k, value):
        wide[pl.ds(k * (det + 1), det)] = value.reshape(det, 8, blk).astype(F32)

    def back_products(k):
        for i in range(0, seg, 2):
            left = jnp.concatenate([wide[index[k, 1, i]], wide[index[k, 1, i + 1]]], axis=0).astype(BF16)
            weight = jnp.concatenate([tiles[index[k, 2, i]], tiles[index[k, 2, i + 1]]], axis=1)
            both = jnp.dot(left, weight, preferred_element_type=F32)
            p = k * seg + i
            terms[pl.ds(p, 8, stride=pairs + 8), :] = both[:8, :blk]
            terms[pl.ds(p + 1, 8, stride=pairs + 8), :] = both[8:, blk:]

    vox_row = lax.broadcasted_iota(jnp.int32, (blocks, seg), 0)

    def scattered(hot, lo, r):
        high, low = split(terms[pl.ds(r * (pairs + 8) + lo * seg, 4 * seg)])
        both = jnp.dot(hot, jnp.concatenate([high, low], axis=1), preferred_element_type=F32)
        return both[:, :blk] + both[:, blk:]

    def hots(lo):
        hot = [jnp.where(vox_row == in_lists[k, 0:1, :], 1.0, 0.0).astype(BF16) for k in range(lo, lo + 4)]
        return jnp.concatenate(hot, axis=1)

    widen(0, q_near[0])

    def near_back(j, _):
        @at_step(j, 1)
        def _():
            around[1].wait_recv()
            around[3].wait_recv()
            widen(1, q_near[1])
            widen(3, q_near[3])

        @at_step(j, 3)
        def _():
            around[2].wait_recv()
            widen(2, q_near[2])

        back_products(turn(j))
        return 0

    lax.fori_loop(0, 4, near_back, 0)
    over.wait_recv()
    for k in (2, 1, 3):
        onward[k].start()
    widen(4, q_far[0])
    hot = hots(0)
    for r in range(8):
        back[pl.ds(r * blocks, blocks)] = scattered(hot, 0, r)

    def far_back(j, _):
        @at_step(j, 1)
        def _():
            onward[1].wait_recv()
            onward[3].wait_recv()
            widen(5, q_far[1])
            widen(7, q_far[3])

        @at_step(j, 3)
        def _():
            onward[2].wait_recv()
            widen(6, q_far[2])

        back_products(4 + turn(j))
        return 0

    lax.fori_loop(0, 4, far_back, 0)
    hot = hots(4)

    def finish(r):
        back[pl.ds(r * blocks, blocks)] += scattered(hot, 4, r)

    finish(0)
    finish(7)
    vol_up[...] += primal_w[1, 2] * back[pl.ds(0, blocks)]
    vol_down[...] += primal_w[1, 0] * back[pl.ds(7 * blocks, blocks)]
    to_next = remote(vol_down, back_prev, vs.at[0], vr.at[0], following)
    to_prev = remote(vol_up, back_next, vs.at[1], vr.at[1], prev)

    @pl.when(has_next)
    def _():
        to_next.start()

    @pl.when(has_prev)
    def _():
        to_prev.start()

    for r in range(1, 7):
        finish(r)

    for r in range(8):
        value = primal_w[1, 1] * back[pl.ds(r * blocks, blocks)]
        if r > 0:
            value = value + primal_w[1, 0] * back[pl.ds((r - 1) * blocks, blocks)]
        if r < 7:
            value = value + primal_w[1, 2] * back[pl.ds((r + 1) * blocks, blocks)]
        terms[pl.ds(r * (blocks + 8), blocks)] = value

    @pl.when(has_prev)
    def _():
        to_next.wait_recv()
        terms[pl.ds(0, blocks)] += back_prev[...]

    @pl.when(has_next)
    def _():
        to_prev.wait_recv()
        terms[pl.ds(7 * (blocks + 8), blocks)] += back_next[...]

    def merge(i, _):
        for u in range(16):
            v = i * 16 + u
            new_vol[v] += terms[pl.ds(v, 8, stride=blocks + 8), :]
        return 0

    lax.fori_loop(0, blocks // 16, merge, 0)

    sent = [list_copies, near_copies, far_copies, around, onward]
    for copy in [copy for group_of in sent for copy in group_of.values()] + [across, over]:
        copy.wait_send()

    @pl.when(has_prev)
    def _():
        far_up.wait_send()
        near_up.wait_send()
        to_prev.wait_send()

    @pl.when(has_next)
    def _():
        far_down.wait_send()
        near_down.wait_send()
        to_next.wait_send()


def store_kernel(vol_ref, dual_ref, vol_out, dual_out, sem):
    copies = [
        pltpu.make_async_copy(source, target, sem.at[i])
        for i, (source, target) in enumerate([(vol_ref, vol_out), (dual_ref, dual_out)])
    ]
    for copy in copies:
        copy.start()
    for copy in copies:
        copy.wait()


def on_device(volume, dual, measured, tiles, lists, live, dual_kernel, primal_kernel):
    groups, slabs = lax.axis_size("angle"), lax.axis_size("slab")
    blocks, _, blk = volume.shape
    width = dual.shape[2]
    det = width // blk
    rows = det * 8
    vmem, smem = pl.BlockSpec(memory_space=pltpu.VMEM), pl.BlockSpec(memory_space=pltpu.SMEM)
    hbm = pl.BlockSpec(memory_space=pl.ANY)
    dma = pltpu.SemaphoreType.DMA
    ramp = jnp.asarray(ramp_matrix(width, blk))
    outs = pl.pallas_call(
        functools.partial(step_kernel, slabs),
        out_shape=[pltpu.VMEM(volume.shape, F32), pltpu.VMEM((8, width), F32)],
        in_specs=[vmem, smem, hbm, hbm, hbm, hbm, hbm, smem, smem],
        out_specs=[vmem, vmem],
        scratch_shapes=[
            pltpu.VMEM(volume.shape, F32),
            pltpu.VMEM((8, width), F32),
            pltpu.VMEM((8, width), F32),
            pltpu.VMEM(tiles.shape, BF16),
            pltpu.VMEM(ramp.shape, BF16),
            pltpu.VMEM((tiles.shape[0] * blocks, 8, blk), F32),
            pltpu.VMEM((blocks * 8, blk), BF16),
            pltpu.VMEM((groups, 8, blk), jnp.int32),
            pltpu.VMEM((groups, 8, blk), jnp.int32),
            pltpu.VMEM((groups, 8, blk), jnp.int32),
            pltpu.SMEM((groups, 8, blk), jnp.int32),
            pltpu.VMEM((10 * blk, blk), F32),
            pltpu.VMEM((8, rows, blk), BF16),
            pltpu.VMEM((3, rows, blk), BF16),
            pltpu.VMEM((3, rows, blk), BF16),
            pltpu.VMEM((rows + det, blk), F32),
            pltpu.VMEM((rows, blk), BF16),
            pltpu.VMEM((rows, blk), BF16),
            pltpu.VMEM((8, width), F32),
        ]
        + [pltpu.VMEM((1, width), F32)] * 4
        + [pltpu.VMEM((det, blk), BF16)] * 2
        + [pltpu.VMEM((2 * rows, blk), BF16)] * 4
        + [pltpu.VMEM((4, rows, blk), BF16)] * 2
        + [
            pltpu.VMEM((groups * (det + 1), 8, blk), F32),
            pltpu.VMEM((9 * (groups * blk + 8), blk), F32),
            pltpu.VMEM((8 * blocks, blk), F32),
        ]
        + [pltpu.VMEM((blocks, blk), F32)] * 4
        + [dma((5,)), dma((7,)), dma((7,)), dma((8,))]
        + [dma((3,))] * 4
        + [dma((1,))] * 2
        + [dma((2,))] * 4
        + [dma((1,))] * 2
        + [dma((3,))] * 4
        + [dma((2,))] * 2,
        compiler_params=pltpu.CompilerParams(
            collective_id=0, has_side_effects=True, vmem_limit_bytes=VMEM_LIMIT
        ),
    )(lists, live, volume, dual[0], measured[0], tiles, ramp, dual_kernel, primal_kernel)
    new_volume, new_dual = pl.pallas_call(
        store_kernel,
        out_shape=[jax.ShapeDtypeStruct(volume.shape, F32), jax.ShapeDtypeStruct((8, width), F32)],
        in_specs=[vmem, vmem],
        out_specs=[hbm, hbm],
        scratch_shapes=[dma((2,))],
    )(*[pltpu.with_memory_space_constraint(out, pltpu.VMEM) for out in outs])
    return (new_volume, new_dual[None])


def solution(mesh):
    in_specs = (
        P("angle", "slab", None),
        P("angle", "slab", None),
        P("angle", "slab", None),
        P(),
        P(None, "slab", "angle"),
        P("slab", "angle"),
        P(),
        P(),
    )
    out_specs = (P("angle", "slab", None), P("angle", "slab", None))
    return jax.shard_map(
        on_device, mesh=mesh, in_specs=in_specs, out_specs=out_specs, check_vma=False
    )
```

```python
import functools

import jax
import jax.numpy as jnp
import ml_dtypes
import numpy as np
from jax import lax
from jax.experimental import pallas as pl
from jax.experimental.pallas import tpu as pltpu
from jax.sharding import PartitionSpec as P

F32 = jnp.float32
BF16 = jnp.bfloat16
MESH = pl.DeviceIdType.MESH
CONTRACT_LAST = (((1,), (1,)), ((), ()))
CONTRACT_INNER = (((1,), (0,)), ((), ()))
VMEM_LIMIT = 56 * 2**20
X_SIZE = 4


def ramp_matrix(width, blk):
    n = np.arange(width)
    taps = np.zeros(width)
    odd = n % 2 == 1
    taps[odd] = -(2.0 / width**2) / np.sin(np.pi * n[odd] / width) ** 2
    k = np.arange(width // blk)[:, None, None]
    i = np.arange(blk)[None, :, None]
    j = np.arange(blk)[None, None, :]
    full = taps[(blk * k + j - i) % width].reshape(width, blk)
    high = full.astype(ml_dtypes.bfloat16)
    low = (full - high.astype(np.float64)).astype(ml_dtypes.bfloat16)
    return np.concatenate([high, low], axis=1)


def remote(src, dst, send, recv, device):
    return pltpu.make_async_remote_copy(
        src_ref=src, dst_ref=dst, send_sem=send, recv_sem=recv, device_id=device, device_id_type=MESH
    )


def step_kernel(
    slabs,
    lists_ref,
    live_ref,
    vol_hbm,
    dual_hbm,
    meas_hbm,
    tiles_hbm,
    ramp_hbm,
    dual_w,
    primal_w,
    new_vol,
    new_dual,
    vol_ref,
    dual_ref,
    meas_ref,
    tiles,
    ramp,
    dense,
    rounded,
    out_lists,
    in_lists,
    prepared,
    index,
    picked,
    picked_too,
    part,
    land_near,
    land_far,
    near,
    send_z,
    land_z,
    misfit,
    down,
    up,
    from_prev,
    from_next,
    far_prev,
    far_next,
    even,
    odd,
    even_low,
    odd_low,
    q_near,
    q_far,
    wide,
    terms,
    back,
    vol_down,
    vol_up,
    back_prev,
    back_next,
    load_sem,
    ls,
    lr,
    index_sem,
    ns,
    nr,
    fs,
    fr,
    zs,
    zr,
    es,
    er,
    ps,
    pr,
    gs,
    gr,
    hs,
    hr,
    ws,
    wr,
    vs,
    vr,
):
    slab, me = lax.axis_index("slab"), lax.axis_index("angle")
    x, z = me // 2, lax.rem(me, 2)
    has_prev, has_next = slab > 0, slab < slabs - 1
    blocks, _, blk = vol_ref.shape
    width = dual_ref.shape[1]
    det = width // blk
    rows = det * 8
    seg = blk
    pairs = 8 * seg
    tile_count = tiles.shape[0]

    def group(k):
        return 2 * lax.rem(x + k % 4, 4) + (1 - z if k >= 4 else z)

    def device(k):
        return (slab, group(k))

    def mirror(k):
        return (4 - k % 4) % 4 + 4 * (k // 4)

    prev, following = (slab - 1, me), (slab + 1, me)
    far_me = 2 * x + 1 - z
    prev_far, following_far = (slab - 1, far_me), (slab + 1, far_me)

    barrier = pltpu.get_barrier_semaphore()
    for k in range(1, 8):
        pl.semaphore_signal(barrier, inc=1, device_id=device(k), device_id_type=MESH)

    @pl.when(has_prev)
    def _():
        pl.semaphore_signal(barrier, inc=1, device_id=prev, device_id_type=MESH)
        pl.semaphore_signal(barrier, inc=1, device_id=prev_far, device_id_type=MESH)

    @pl.when(has_next)
    def _():
        pl.semaphore_signal(barrier, inc=1, device_id=following, device_id_type=MESH)
        pl.semaphore_signal(barrier, inc=1, device_id=following_far, device_id_type=MESH)

    loads = [
        pltpu.make_async_copy(source, target, load_sem.at[i])
        for i, (source, target) in enumerate(
            [(tiles_hbm, tiles), (vol_hbm, vol_ref), (dual_hbm, dual_ref), (meas_hbm, meas_ref), (ramp_hbm, ramp)]
        )
    ]
    for load in loads:
        load.start()

    lane = lax.broadcasted_iota(jnp.int32, (1, seg), 1)
    for j in range(8):
        cols = pl.ds(j * seg, seg)
        out_lists[j, 0:1, :] = jnp.clip(lists_ref[0, :, cols] - j * blocks, 0, blocks - 1)
        out_lists[j, 1:2, :] = jnp.where(lane < live_ref[0, j], lists_ref[1, :, cols], det)
        out_lists[j, 2:3, :] = lists_ref[2, :, cols]
        out_lists[j, 3:8, :] = jnp.zeros((5, seg), jnp.int32)

    def prepare(k):
        voxel, detector, tile = in_lists[k, 0:1, :], in_lists[k, 1:2, :], in_lists[k, 2:3, :]
        prepared[k, 0:1, :] = tile * blocks + voxel
        prepared[k, 1:2, :] = detector + k * (det + 1)
        prepared[k, 2:8, :] = in_lists[k, 2:8, :]
        copy = pltpu.make_async_copy(prepared.at[k], index.at[k], index_sem.at[k])
        copy.start()
        return copy

    in_lists[0] = out_lists[me]
    own_index = prepare(0)
    loads[0].wait()
    loads[1].wait()
    rounded[...] = vol_ref[...].reshape(blocks * 8, blk).astype(BF16)

    def products(i, _):
        for u in range(0, 8, 2):
            t = i * 8 + u
            both = lax.dot_general(
                rounded[...], tiles[pl.ds(t, 2)].reshape(2 * blk, blk), CONTRACT_LAST, preferred_element_type=F32
            )
            dense[pl.ds(t * blocks, blocks)] = both[:, :blk].reshape(blocks, 8, blk)
            dense[pl.ds((t + 1) * blocks, blocks)] = both[:, blk:].reshape(blocks, 8, blk)
        return 0

    early = tile_count // 8 - 4
    lax.fori_loop(0, early, products, 0)
    present = 2 * (has_prev.astype(jnp.int32) + has_next.astype(jnp.int32))
    pl.semaphore_wait(barrier, 7 + present)

    list_copies = {}
    for k in (6, 5, 7, 4, 2, 1, 3):
        list_copies[k] = remote(
            out_lists.at[group(k)], in_lists.at[mirror(k)], ls.at[k - 1], lr.at[mirror(k) - 1], device(k)
        )
        list_copies[k].start()
    lax.fori_loop(early, tile_count // 8, products, 0)

    def split(value):
        high = value.astype(BF16)
        return high, (value - high.astype(F32)).astype(BF16)

    det_row = lax.broadcasted_iota(jnp.int32, (det, seg), 0)

    sides = (picked, picked_too)

    def project(k, side, after=None):
        parts = []
        for r in range(8):
            if after is not None:
                for i in range(r * seg // 8, (r + 1) * seg // 8):
                    sides[1 - side][pl.ds(i, 8, stride=seg + 8), :] = dense[index[after, 0, i]]
            if k is not None:
                parts.append(split(sides[side][pl.ds(r * (seg + 8), seg)]))
        if k is None:
            return
        stacked = jnp.concatenate(
            [jnp.concatenate([p[0] for p in parts], axis=1), jnp.concatenate([p[1] for p in parts], axis=1)], axis=0
        )
        hot = jnp.where(det_row == in_lists[k, 1:2, :], 1.0, 0.0).astype(BF16)
        summed = jnp.dot(jnp.concatenate([hot, hot], axis=1), stacked, preferred_element_type=F32)
        for r in range(8):
            here = pl.ds(r * det, det)
            value = summed[:, r * blk : (r + 1) * blk]
            if k == 0:
                near[here] = value
            else:
                part[k, here] = value.astype(BF16)

    def turn(j):
        return lax.rem(j * (j + 1) // 2, 4)

    near_copies = {
        d: remote(part.at[d], land_near.at[mirror(d) - 1], ns.at[d - 1], nr.at[mirror(d) - 1], device(d))
        for d in (1, 3, 2)
    }
    far_copies = {
        d: remote(part.at[d + 4], land_far.at[mirror(d) - 1], fs.at[d - 1], fr.at[mirror(d) - 1], device(d))
        for d in (2, 3, 1)
    }

    def at_step(j, step):
        return pl.when(j == step)

    def receive(ks):
        for k in ks:
            list_copies[k].wait_recv()
        copies = [prepare(k) for k in ks]
        for copy in copies:
            copy.wait()

    own_index.wait()
    project(None, 1, 0)
    receive((1, 3, 2))
    project(0, 0, 1)
    project(1, 1, 3)
    near_copies[1].start()
    project(3, 0, 2)
    near_copies[3].start()
    project(2, 1)
    near_copies[2].start()
    receive((4, 5, 7, 6))
    project(None, 1, 6)
    project(6, 0, 7)
    far_copies[2].start()
    project(7, 1, 5)
    far_copies[3].start()
    project(5, 0, 4)
    far_copies[1].start()
    project(4, 1)

    for copy in far_copies.values():
        copy.wait_recv()
    total = part[4].astype(F32)
    for d in range(3):
        total = total + land_far[d].astype(F32)
    send_z[...] = total.astype(BF16)
    across = remote(send_z, land_z, zs.at[0], zr.at[0], device(4))
    across.start()
    first, last = pl.ds(0, det), pl.ds(rows - det, det)
    far_up = remote(send_z.at[first], far_next, ps.at[0], pr.at[0], prev_far)
    far_down = remote(send_z.at[last], far_prev, ps.at[1], pr.at[1], following_far)

    @pl.when(has_prev)
    def _():
        far_up.start()

    @pl.when(has_next)
    def _():
        far_down.start()

    loads[2].wait()
    loads[3].wait()
    for copy in near_copies.values():
        copy.wait_recv()
    whole = pl.ds(0, rows)
    total = near[whole]
    for d in range(3):
        total = total + land_near[d].astype(F32)
    near[whole] = total
    for b in range(det):
        cols = pl.ds(b * blk, blk)
        misfit[:, cols] = near[pl.ds(b, 8, stride=det), :] - meas_ref[:, cols]
    down[...] = dual_w[0, 0] * dual_ref[7:8, :] + dual_w[1, 0] * misfit[7:8, :]
    up[...] = dual_w[0, 2] * dual_ref[0:1, :] + dual_w[1, 2] * misfit[0:1, :]
    near_down = remote(down, from_prev, es.at[0], er.at[0], following)
    near_up = remote(up, from_next, es.at[1], er.at[1], prev)

    @pl.when(has_next)
    def _():
        near_down.start()

    @pl.when(has_prev)
    def _():
        near_up.start()

    vol_down[...] = vol_ref[:, 7, :] * primal_w[0, 0]
    vol_up[...] = vol_ref[:, 0, :] * primal_w[0, 2]
    for k in range(8):
        wide[k * (det + 1) + det] = jnp.zeros((8, blk), F32)
    row = lax.broadcasted_iota(jnp.int32, (1, 8, blk), 1)

    def volume_part(i, _):
        here = pl.ds(i * 8, 8)
        vol = vol_ref[here]
        before = jnp.where(row == 0, 0.0, pltpu.roll(primal_w[0, 0] * vol, 1, 1))
        after = jnp.where(row == 7, 0.0, pltpu.roll(primal_w[0, 2] * vol, 7, 1))
        new_vol[here] = vol + primal_w[0, 1] * vol + before + after
        return 0

    lax.fori_loop(0, blocks // 8, volume_part, 0)
    loads[4].wait()

    @pl.when(has_prev)
    def _():
        near_down.wait_recv()
        far_down.wait_recv()

    @pl.when(jnp.logical_not(has_prev))
    def _():
        from_prev[...] = jnp.zeros_like(from_prev)
        far_prev[...] = jnp.zeros_like(far_prev)

    @pl.when(has_next)
    def _():
        near_up.wait_recv()
        far_up.wait_recv()

    @pl.when(jnp.logical_not(has_next))
    def _():
        from_next[...] = jnp.zeros_like(from_next)
        far_next[...] = jnp.zeros_like(far_next)

    across.wait_recv()
    near[whole] = land_z[...].astype(F32)
    flat_row = lax.broadcasted_iota(jnp.int32, (8, blk), 0)
    before_far = far_prev[...].astype(F32) * dual_w[1, 0]
    after_far = far_next[...].astype(F32) * dual_w[1, 2]

    def updated(b):
        cols = pl.ds(b * blk, blk)
        dual = dual_ref[:, cols]
        mis = misfit[:, cols] + near[pl.ds(b, 8, stride=det), :]
        before = pltpu.roll(dual_w[0, 0] * dual + dual_w[1, 0] * mis, 1, 0)
        after = pltpu.roll(dual_w[0, 2] * dual + dual_w[1, 2] * mis, 7, 0)
        before = jnp.where(flat_row == 0, from_prev[:, cols] + before_far[b : b + 1], before)
        after = jnp.where(flat_row == 7, from_next[:, cols] + after_far[b : b + 1], after)
        new = dual + dual_w[0, 1] * dual + dual_w[1, 1] * mis + before + after
        new_dual[:, cols] = new
        return new

    news = [updated(b) for b in range(det)]
    for b in range(det):
        high, low = split(jnp.concatenate([news[b], news[(b + 1) % det]], axis=0))
        for base in (0, rows):
            if b % 2 == 0:
                even[pl.ds(base + b * 8, 16)] = high
                even_low[pl.ds(base + b * 8, 16)] = low
            else:
                odd[pl.ds(base + (b - 1) * 8, 16)] = high
                odd_low[pl.ds(base + (b - 1) * 8, 16)] = low
    total = jnp.zeros((rows, 2 * blk), F32)
    small = jnp.zeros((rows, blk), F32)
    for k in range(0, det, 2):
        here = pl.ds((det - k) * 8 % rows, rows)
        there = pl.ds((det - k - 2) * 8, rows)
        weight = ramp[pl.ds(k * blk, 2 * blk)]
        high = jnp.concatenate([even[here], odd[there]], axis=1)
        low = jnp.concatenate([even_low[here], odd_low[there]], axis=1)
        total = total + jnp.dot(high, weight, preferred_element_type=F32)
        small = small + jnp.dot(low, weight[:, :blk], preferred_element_type=F32)
    small = small + total[:, blk:] + total[:, :blk]
    for b in range(0, det, 2):
        both = jnp.concatenate([new_dual[:, pl.ds(b * blk, blk)], new_dual[:, pl.ds((b + 1) * blk, blk)]], axis=0)
        q_near[0, pl.ds(b * 8, 16)] = (0.5 * both + small[b * 8 : b * 8 + 16]).astype(BF16)

    step = rows // 2
    halves = [pl.ds(0, step), pl.ds(step, step)]
    over = []
    for c, half in enumerate(halves):
        over.append(remote(q_near.at[0, half], q_far.at[0, half], gs.at[c], gr.at[c], device(4)))
        over[c].start()
    around, onward = {}, {}
    for k in (2, 1, 3):
        around[k] = remote(q_near.at[0], q_near.at[mirror(k)], hs.at[k - 1], hr.at[mirror(k) - 1], device(k))
        around[k].start()
        for c, half in enumerate(halves):
            onward[k, c] = remote(
                q_far.at[0, half], q_far.at[mirror(k), half], ws.at[k - 1, c], wr.at[mirror(k) - 1, c], device(k)
            )

    def widen(k, value):
        wide[pl.ds(k * (det + 1), det)] = value.reshape(det, 8, blk).astype(F32)

    def back_products(k):
        for i in range(0, seg, 2):
            left = jnp.concatenate([wide[index[k, 1, i]], wide[index[k, 1, i + 1]]], axis=0).astype(BF16)
            weight = jnp.concatenate([tiles[index[k, 2, i]], tiles[index[k, 2, i + 1]]], axis=1)
            both = jnp.dot(left, weight, preferred_element_type=F32)
            p = k * seg + i
            terms[pl.ds(p, 8, stride=pairs + 8), :] = both[:8, :blk]
            terms[pl.ds(p + 1, 8, stride=pairs + 8), :] = both[8:, blk:]

    vox_row = lax.broadcasted_iota(jnp.int32, (blocks, seg), 0)

    def scattered(hot, lo, r):
        high, low = split(terms[pl.ds(r * (pairs + 8) + lo * seg, 4 * seg)])
        both = jnp.dot(hot, jnp.concatenate([high, low], axis=1), preferred_element_type=F32)
        return both[:, :blk] + both[:, blk:]

    def hots(lo):
        hot = [jnp.where(vox_row == in_lists[k, 0:1, :], 1.0, 0.0).astype(BF16) for k in range(lo, lo + 4)]
        return jnp.concatenate(hot, axis=1)

    widen(0, q_near[0])

    def near_back(j, _):
        @at_step(j, 1)
        def _():
            around[1].wait_recv()
            around[3].wait_recv()
            widen(1, q_near[1])
            widen(3, q_near[3])

        @at_step(j, 3)
        def _():
            around[2].wait_recv()
            widen(2, q_near[2])

        back_products(turn(j))
        return 0

    lax.fori_loop(0, 4, near_back, 0)
    for c in range(2):
        over[c].wait_recv()
        for k in (2, 1, 3):
            onward[k, c].start()
    widen(4, q_far[0])
    hot = hots(0)
    for r in range(8):
        back[pl.ds(r * blocks, blocks)] = scattered(hot, 0, r)

    def far_back(j, _):
        @at_step(j, 1)
        def _():
            for k, c in ((1, 0), (3, 0), (1, 1), (3, 1)):
                onward[k, c].wait_recv()
            widen(5, q_far[1])
            widen(7, q_far[3])

        @at_step(j, 3)
        def _():
            for c in range(2):
                onward[2, c].wait_recv()
            widen(6, q_far[2])

        back_products(4 + turn(j))
        return 0

    lax.fori_loop(0, 4, far_back, 0)
    hot = hots(4)

    def finish(r):
        back[pl.ds(r * blocks, blocks)] += scattered(hot, 4, r)

    finish(0)
    finish(7)
    vol_up[...] += primal_w[1, 2] * back[pl.ds(0, blocks)]
    vol_down[...] += primal_w[1, 0] * back[pl.ds(7 * blocks, blocks)]
    to_next = remote(vol_down, back_prev, vs.at[0], vr.at[0], following)
    to_prev = remote(vol_up, back_next, vs.at[1], vr.at[1], prev)

    @pl.when(has_next)
    def _():
        to_next.start()

    @pl.when(has_prev)
    def _():
        to_prev.start()

    for r in range(1, 7):
        finish(r)

    for r in range(8):
        value = primal_w[1, 1] * back[pl.ds(r * blocks, blocks)]
        if r > 0:
            value = value + primal_w[1, 0] * back[pl.ds((r - 1) * blocks, blocks)]
        if r < 7:
            value = value + primal_w[1, 2] * back[pl.ds((r + 1) * blocks, blocks)]
        terms[pl.ds(r * (blocks + 8), blocks)] = value

    @pl.when(has_prev)
    def _():
        to_next.wait_recv()
        terms[pl.ds(0, blocks)] += back_prev[...]

    @pl.when(has_next)
    def _():
        to_prev.wait_recv()
        terms[pl.ds(7 * (blocks + 8), blocks)] += back_next[...]

    def merge(i, _):
        for u in range(16):
            v = i * 16 + u
            new_vol[v] += terms[pl.ds(v, 8, stride=blocks + 8), :]
        return 0

    lax.fori_loop(0, blocks // 16, merge, 0)

    sent = [list_copies, near_copies, far_copies, around, onward]
    for copy in [copy for group_of in sent for copy in group_of.values()] + [across] + over:
        copy.wait_send()

    @pl.when(has_prev)
    def _():
        far_up.wait_send()
        near_up.wait_send()
        to_prev.wait_send()

    @pl.when(has_next)
    def _():
        far_down.wait_send()
        near_down.wait_send()
        to_next.wait_send()


def store_kernel(vol_ref, dual_ref, vol_out, dual_out, sem):
    copies = [
        pltpu.make_async_copy(source, target, sem.at[i])
        for i, (source, target) in enumerate([(vol_ref, vol_out), (dual_ref, dual_out)])
    ]
    for copy in copies:
        copy.start()
    for copy in copies:
        copy.wait()


def on_device(volume, dual, measured, tiles, lists, live, dual_kernel, primal_kernel):
    groups, slabs = lax.axis_size("angle"), lax.axis_size("slab")
    blocks, _, blk = volume.shape
    width = dual.shape[2]
    det = width // blk
    rows = det * 8
    vmem, smem = pl.BlockSpec(memory_space=pltpu.VMEM), pl.BlockSpec(memory_space=pltpu.SMEM)
    hbm = pl.BlockSpec(memory_space=pl.ANY)
    dma = pltpu.SemaphoreType.DMA
    ramp = jnp.asarray(ramp_matrix(width, blk))
    outs = pl.pallas_call(
        functools.partial(step_kernel, slabs),
        out_shape=[pltpu.VMEM(volume.shape, F32), pltpu.VMEM((8, width), F32)],
        in_specs=[vmem, smem, hbm, hbm, hbm, hbm, hbm, smem, smem],
        out_specs=[vmem, vmem],
        scratch_shapes=[
            pltpu.VMEM(volume.shape, F32),
            pltpu.VMEM((8, width), F32),
            pltpu.VMEM((8, width), F32),
            pltpu.VMEM(tiles.shape, BF16),
            pltpu.VMEM(ramp.shape, BF16),
            pltpu.VMEM((tiles.shape[0] * blocks, 8, blk), F32),
            pltpu.VMEM((blocks * 8, blk), BF16),
            pltpu.VMEM((groups, 8, blk), jnp.int32),
            pltpu.VMEM((groups, 8, blk), jnp.int32),
            pltpu.VMEM((groups, 8, blk), jnp.int32),
            pltpu.SMEM((groups, 8, blk), jnp.int32),
            pltpu.VMEM((10 * blk, blk), F32),
            pltpu.VMEM((10 * blk, blk), F32),
            pltpu.VMEM((8, rows, blk), BF16),
            pltpu.VMEM((3, rows, blk), BF16),
            pltpu.VMEM((3, rows, blk), BF16),
            pltpu.VMEM((rows + det, blk), F32),
            pltpu.VMEM((rows, blk), BF16),
            pltpu.VMEM((rows, blk), BF16),
            pltpu.VMEM((8, width), F32),
        ]
        + [pltpu.VMEM((1, width), F32)] * 4
        + [pltpu.VMEM((det, blk), BF16)] * 2
        + [pltpu.VMEM((2 * rows, blk), BF16)] * 4
        + [pltpu.VMEM((4, rows, blk), BF16)] * 2
        + [
            pltpu.VMEM((groups * (det + 1), 8, blk), F32),
            pltpu.VMEM((9 * (groups * blk + 8), blk), F32),
            pltpu.VMEM((8 * blocks, blk), F32),
        ]
        + [pltpu.VMEM((blocks, blk), F32)] * 4
        + [dma((5,)), dma((7,)), dma((7,)), dma((8,))]
        + [dma((3,))] * 4
        + [dma((1,))] * 2
        + [dma((2,))] * 6
        + [dma((3,))] * 2
        + [dma((3, 2))] * 2
        + [dma((2,))] * 2,
        compiler_params=pltpu.CompilerParams(
            collective_id=0, has_side_effects=True, vmem_limit_bytes=VMEM_LIMIT
        ),
    )(lists, live, volume, dual[0], measured[0], tiles, ramp, dual_kernel, primal_kernel)
    new_volume, new_dual = pl.pallas_call(
        store_kernel,
        out_shape=[jax.ShapeDtypeStruct(volume.shape, F32), jax.ShapeDtypeStruct((8, width), F32)],
        in_specs=[vmem, vmem],
        out_specs=[hbm, hbm],
        scratch_shapes=[dma((2,))],
    )(*[pltpu.with_memory_space_constraint(out, pltpu.VMEM) for out in outs])
    return (new_volume, new_dual[None])


def solution(mesh):
    in_specs = (
        P("angle", "slab", None),
        P("angle", "slab", None),
        P("angle", "slab", None),
        P(),
        P(None, "slab", "angle"),
        P("slab", "angle"),
        P(),
        P(),
    )
    out_specs = (P("angle", "slab", None), P("angle", "slab", None))
    return jax.shard_map(
        on_device, mesh=mesh, in_specs=in_specs, out_specs=out_specs, check_vma=False
    )
```

```python
import functools

import jax
import jax.numpy as jnp
import ml_dtypes
import numpy as np
from jax import lax
from jax.experimental import pallas as pl
from jax.experimental.pallas import tpu as pltpu
from jax.sharding import PartitionSpec as P

F32 = jnp.float32
BF16 = jnp.bfloat16
MESH = pl.DeviceIdType.MESH
CONTRACT_LAST = (((1,), (1,)), ((), ()))
CONTRACT_INNER = (((1,), (0,)), ((), ()))
VMEM_LIMIT = 56 * 2**20
X_SIZE = 4


def ramp_matrix(width, blk):
    n = np.arange(width)
    taps = np.zeros(width)
    odd = n % 2 == 1
    taps[odd] = -(2.0 / width**2) / np.sin(np.pi * n[odd] / width) ** 2
    k = np.arange(width // blk)[:, None, None]
    i = np.arange(blk)[None, :, None]
    j = np.arange(blk)[None, None, :]
    full = taps[(blk * k + j - i) % width].reshape(width, blk)
    high = full.astype(ml_dtypes.bfloat16)
    low = (full - high.astype(np.float64)).astype(ml_dtypes.bfloat16)
    return np.concatenate([high, low], axis=1)


def remote(src, dst, send, recv, device):
    return pltpu.make_async_remote_copy(
        src_ref=src, dst_ref=dst, send_sem=send, recv_sem=recv, device_id=device, device_id_type=MESH
    )


def step_kernel(
    slabs,
    lists_hbm,
    live_hbm,
    vol_hbm,
    dual_hbm,
    meas_hbm,
    tiles_hbm,
    ramp_hbm,
    dual_w_hbm,
    primal_w_hbm,
    new_vol,
    new_dual,
    lists_ref,
    live_ref,
    dual_w,
    primal_w,
    vol_ref,
    dual_ref,
    meas_ref,
    tiles,
    ramp,
    dense,
    rounded,
    out_lists,
    in_lists,
    prepared,
    index,
    picked,
    picked_too,
    part,
    land_near,
    land_far,
    near,
    send_z,
    land_z,
    misfit,
    down,
    up,
    from_prev,
    from_next,
    far_prev,
    far_next,
    even,
    odd,
    even_low,
    odd_low,
    q_near,
    q_far,
    wide,
    terms,
    back,
    vol_down,
    vol_up,
    back_prev,
    back_next,
    small_sem,
    load_sem,
    ls,
    lr,
    index_sem,
    ns,
    nr,
    fs,
    fr,
    zs,
    zr,
    es,
    er,
    ps,
    pr,
    gs,
    gr,
    hs,
    hr,
    ws,
    wr,
    vs,
    vr,
):
    slab, me = lax.axis_index("slab"), lax.axis_index("angle")
    x, z = me // 2, lax.rem(me, 2)
    has_prev, has_next = slab > 0, slab < slabs - 1
    blocks, _, blk = vol_ref.shape
    width = dual_ref.shape[1]
    det = width // blk
    rows = det * 8
    seg = blk
    pairs = 8 * seg
    tile_count = tiles.shape[0]

    def group(k):
        return 2 * lax.rem(x + k % 4, 4) + (1 - z if k >= 4 else z)

    def device(k):
        return (slab, group(k))

    def mirror(k):
        return (4 - k % 4) % 4 + 4 * (k // 4)

    prev, following = (slab - 1, me), (slab + 1, me)
    far_me = 2 * x + 1 - z
    prev_far, following_far = (slab - 1, far_me), (slab + 1, far_me)

    barrier = pltpu.get_barrier_semaphore()
    for k in range(1, 8):
        pl.semaphore_signal(barrier, inc=1, device_id=device(k), device_id_type=MESH)

    @pl.when(has_prev)
    def _():
        pl.semaphore_signal(barrier, inc=1, device_id=prev, device_id_type=MESH)
        pl.semaphore_signal(barrier, inc=1, device_id=prev_far, device_id_type=MESH)

    @pl.when(has_next)
    def _():
        pl.semaphore_signal(barrier, inc=1, device_id=following, device_id_type=MESH)
        pl.semaphore_signal(barrier, inc=1, device_id=following_far, device_id_type=MESH)

    small = [
        pltpu.make_async_copy(source, target, small_sem.at[i])
        for i, (source, target) in enumerate(
            [(lists_hbm, lists_ref), (live_hbm, live_ref), (dual_w_hbm, dual_w), (primal_w_hbm, primal_w)]
        )
    ]
    for load in small:
        load.start()
    loads = [
        pltpu.make_async_copy(source, target, load_sem.at[i])
        for i, (source, target) in enumerate(
            [(tiles_hbm, tiles), (vol_hbm, vol_ref), (dual_hbm, dual_ref), (meas_hbm, meas_ref), (ramp_hbm, ramp)]
        )
    ]
    for load in loads:
        load.start()

    for load in small:
        load.wait()
    lane = lax.broadcasted_iota(jnp.int32, (1, seg), 1)
    for j in range(8):
        cols = pl.ds(j * seg, seg)
        out_lists[j, 0:1, :] = jnp.clip(lists_ref[0, :, cols] - j * blocks, 0, blocks - 1)
        out_lists[j, 1:2, :] = jnp.where(lane < live_ref[0, j], lists_ref[1, :, cols], det)
        out_lists[j, 2:3, :] = lists_ref[2, :, cols]
        out_lists[j, 3:8, :] = jnp.zeros((5, seg), jnp.int32)

    def prepare(k):
        voxel, detector, tile = in_lists[k, 0:1, :], in_lists[k, 1:2, :], in_lists[k, 2:3, :]
        prepared[k, 0:1, :] = tile * blocks + voxel
        prepared[k, 1:2, :] = detector + k * (det + 1)
        prepared[k, 2:8, :] = in_lists[k, 2:8, :]
        copy = pltpu.make_async_copy(prepared.at[k], index.at[k], index_sem.at[k])
        copy.start()
        return copy

    in_lists[0] = out_lists[me]
    own_index = prepare(0)
    loads[0].wait()
    loads[1].wait()
    rounded[...] = vol_ref[...].reshape(blocks * 8, blk).astype(BF16)

    def products(i, _):
        for u in range(0, 8, 2):
            t = i * 8 + u
            both = lax.dot_general(
                rounded[...], tiles[pl.ds(t, 2)].reshape(2 * blk, blk), CONTRACT_LAST, preferred_element_type=F32
            )
            dense[pl.ds(t * blocks, blocks)] = both[:, :blk].reshape(blocks, 8, blk)
            dense[pl.ds((t + 1) * blocks, blocks)] = both[:, blk:].reshape(blocks, 8, blk)
        return 0

    early = tile_count // 8 - 4
    lax.fori_loop(0, early, products, 0)
    present = 2 * (has_prev.astype(jnp.int32) + has_next.astype(jnp.int32))
    pl.semaphore_wait(barrier, 7 + present)

    list_copies = {}
    for k in (6, 5, 7, 4, 2, 1, 3):
        list_copies[k] = remote(
            out_lists.at[group(k)], in_lists.at[mirror(k)], ls.at[k - 1], lr.at[mirror(k) - 1], device(k)
        )
        list_copies[k].start()
    lax.fori_loop(early, tile_count // 8, products, 0)

    def split(value):
        high = value.astype(BF16)
        return high, (value - high.astype(F32)).astype(BF16)

    det_row = lax.broadcasted_iota(jnp.int32, (det, seg), 0)

    sides = (picked, picked_too)

    def project(k, side, after=None):
        parts = []
        for r in range(8):
            if after is not None:
                for i in range(r * seg // 8, (r + 1) * seg // 8):
                    sides[1 - side][pl.ds(i, 8, stride=seg + 8), :] = dense[index[after, 0, i]]
            if k is not None:
                parts.append(split(sides[side][pl.ds(r * (seg + 8), seg)]))
        if k is None:
            return
        stacked = jnp.concatenate(
            [jnp.concatenate([p[0] for p in parts], axis=1), jnp.concatenate([p[1] for p in parts], axis=1)], axis=0
        )
        hot = jnp.where(det_row == in_lists[k, 1:2, :], 1.0, 0.0).astype(BF16)
        summed = jnp.dot(jnp.concatenate([hot, hot], axis=1), stacked, preferred_element_type=F32)
        for r in range(8):
            here = pl.ds(r * det, det)
            value = summed[:, r * blk : (r + 1) * blk]
            if k == 0:
                near[here] = value
            else:
                part[k, here] = value.astype(BF16)

    def turn(j):
        return lax.rem(j * (j + 1) // 2, 4)

    near_copies = {
        d: remote(part.at[d], land_near.at[mirror(d) - 1], ns.at[d - 1], nr.at[mirror(d) - 1], device(d))
        for d in (1, 3, 2)
    }
    far_copies = {
        d: remote(part.at[d + 4], land_far.at[mirror(d) - 1], fs.at[d - 1], fr.at[mirror(d) - 1], device(d))
        for d in (2, 3, 1)
    }

    def at_step(j, step):
        return pl.when(j == step)

    def receive(ks):
        for k in ks:
            list_copies[k].wait_recv()
        copies = [prepare(k) for k in ks]
        for copy in copies:
            copy.wait()

    own_index.wait()
    project(None, 1, 0)
    receive((1, 3, 2))
    project(0, 0, 1)
    project(1, 1, 3)
    near_copies[1].start()
    project(3, 0, 2)
    near_copies[3].start()
    project(2, 1)
    near_copies[2].start()
    receive((4, 5, 7, 6))
    project(None, 1, 6)
    project(6, 0, 7)
    far_copies[2].start()
    project(7, 1, 5)
    far_copies[3].start()
    project(5, 0, 4)
    far_copies[1].start()
    project(4, 1)

    for copy in far_copies.values():
        copy.wait_recv()
    total = part[4].astype(F32)
    for d in range(3):
        total = total + land_far[d].astype(F32)
    send_z[...] = total.astype(BF16)
    across = remote(send_z, land_z, zs.at[0], zr.at[0], device(4))
    across.start()
    first, last = pl.ds(0, det), pl.ds(rows - det, det)
    far_up = remote(send_z.at[first], far_next, ps.at[0], pr.at[0], prev_far)
    far_down = remote(send_z.at[last], far_prev, ps.at[1], pr.at[1], following_far)

    @pl.when(has_prev)
    def _():
        far_up.start()

    @pl.when(has_next)
    def _():
        far_down.start()

    loads[2].wait()
    loads[3].wait()
    for copy in near_copies.values():
        copy.wait_recv()
    whole = pl.ds(0, rows)
    total = near[whole]
    for d in range(3):
        total = total + land_near[d].astype(F32)
    near[whole] = total
    for b in range(det):
        cols = pl.ds(b * blk, blk)
        misfit[:, cols] = near[pl.ds(b, 8, stride=det), :] - meas_ref[:, cols]
    down[...] = dual_w[0, 0] * dual_ref[7:8, :] + dual_w[1, 0] * misfit[7:8, :]
    up[...] = dual_w[0, 2] * dual_ref[0:1, :] + dual_w[1, 2] * misfit[0:1, :]
    near_down = remote(down, from_prev, es.at[0], er.at[0], following)
    near_up = remote(up, from_next, es.at[1], er.at[1], prev)

    @pl.when(has_next)
    def _():
        near_down.start()

    @pl.when(has_prev)
    def _():
        near_up.start()

    vol_down[...] = vol_ref[:, 7, :] * primal_w[0, 0]
    vol_up[...] = vol_ref[:, 0, :] * primal_w[0, 2]
    for k in range(8):
        wide[k * (det + 1) + det] = jnp.zeros((8, blk), F32)
    row = lax.broadcasted_iota(jnp.int32, (1, 8, blk), 1)

    def volume_part(i, _):
        here = pl.ds(i * 8, 8)
        vol = vol_ref[here]
        before = jnp.where(row == 0, 0.0, pltpu.roll(primal_w[0, 0] * vol, 1, 1))
        after = jnp.where(row == 7, 0.0, pltpu.roll(primal_w[0, 2] * vol, 7, 1))
        new_vol[here] = vol + primal_w[0, 1] * vol + before + after
        return 0

    lax.fori_loop(0, blocks // 8, volume_part, 0)
    loads[4].wait()

    @pl.when(has_prev)
    def _():
        near_down.wait_recv()
        far_down.wait_recv()

    @pl.when(jnp.logical_not(has_prev))
    def _():
        from_prev[...] = jnp.zeros_like(from_prev)
        far_prev[...] = jnp.zeros_like(far_prev)

    @pl.when(has_next)
    def _():
        near_up.wait_recv()
        far_up.wait_recv()

    @pl.when(jnp.logical_not(has_next))
    def _():
        from_next[...] = jnp.zeros_like(from_next)
        far_next[...] = jnp.zeros_like(far_next)

    across.wait_recv()
    near[whole] = land_z[...].astype(F32)
    flat_row = lax.broadcasted_iota(jnp.int32, (8, blk), 0)
    before_far = far_prev[...].astype(F32) * dual_w[1, 0]
    after_far = far_next[...].astype(F32) * dual_w[1, 2]

    def updated(b):
        cols = pl.ds(b * blk, blk)
        dual = dual_ref[:, cols]
        mis = misfit[:, cols] + near[pl.ds(b, 8, stride=det), :]
        before = pltpu.roll(dual_w[0, 0] * dual + dual_w[1, 0] * mis, 1, 0)
        after = pltpu.roll(dual_w[0, 2] * dual + dual_w[1, 2] * mis, 7, 0)
        before = jnp.where(flat_row == 0, from_prev[:, cols] + before_far[b : b + 1], before)
        after = jnp.where(flat_row == 7, from_next[:, cols] + after_far[b : b + 1], after)
        new = dual + dual_w[0, 1] * dual + dual_w[1, 1] * mis + before + after
        new_dual[:, cols] = new
        return new

    news = [updated(b) for b in range(det)]
    for b in range(det):
        high, low = split(jnp.concatenate([news[b], news[(b + 1) % det]], axis=0))
        for base in (0, rows):
            if b % 2 == 0:
                even[pl.ds(base + b * 8, 16)] = high
                even_low[pl.ds(base + b * 8, 16)] = low
            else:
                odd[pl.ds(base + (b - 1) * 8, 16)] = high
                odd_low[pl.ds(base + (b - 1) * 8, 16)] = low
    total = jnp.zeros((rows, 2 * blk), F32)
    small = jnp.zeros((rows, blk), F32)
    for k in range(0, det, 2):
        here = pl.ds((det - k) * 8 % rows, rows)
        there = pl.ds((det - k - 2) * 8, rows)
        weight = ramp[pl.ds(k * blk, 2 * blk)]
        high = jnp.concatenate([even[here], odd[there]], axis=1)
        low = jnp.concatenate([even_low[here], odd_low[there]], axis=1)
        total = total + jnp.dot(high, weight, preferred_element_type=F32)
        small = small + jnp.dot(low, weight[:, :blk], preferred_element_type=F32)
    small = small + total[:, blk:] + total[:, :blk]
    for b in range(0, det, 2):
        both = jnp.concatenate([new_dual[:, pl.ds(b * blk, blk)], new_dual[:, pl.ds((b + 1) * blk, blk)]], axis=0)
        q_near[0, pl.ds(b * 8, 16)] = (0.5 * both + small[b * 8 : b * 8 + 16]).astype(BF16)

    step = rows // 2
    halves = [pl.ds(0, step), pl.ds(step, step)]
    over = []
    for c, half in enumerate(halves):
        over.append(remote(q_near.at[0, half], q_far.at[0, half], gs.at[c], gr.at[c], device(4)))
        over[c].start()
    around, onward = {}, {}
    for k in (2, 1, 3):
        around[k] = remote(q_near.at[0], q_near.at[mirror(k)], hs.at[k - 1], hr.at[mirror(k) - 1], device(k))
        around[k].start()
        for c, half in enumerate(halves):
            onward[k, c] = remote(
                q_far.at[0, half], q_far.at[mirror(k), half], ws.at[k - 1, c], wr.at[mirror(k) - 1, c], device(k)
            )

    def widen(k, value):
        wide[pl.ds(k * (det + 1), det)] = value.reshape(det, 8, blk).astype(F32)

    def back_products(k):
        for i in range(0, seg, 2):
            left = jnp.concatenate([wide[index[k, 1, i]], wide[index[k, 1, i + 1]]], axis=0).astype(BF16)
            weight = jnp.concatenate([tiles[index[k, 2, i]], tiles[index[k, 2, i + 1]]], axis=1)
            both = jnp.dot(left, weight, preferred_element_type=F32)
            p = k * seg + i
            terms[pl.ds(p, 8, stride=pairs + 8), :] = both[:8, :blk]
            terms[pl.ds(p + 1, 8, stride=pairs + 8), :] = both[8:, blk:]

    vox_row = lax.broadcasted_iota(jnp.int32, (blocks, seg), 0)

    def scattered(hot, lo, r):
        high, low = split(terms[pl.ds(r * (pairs + 8) + lo * seg, 4 * seg)])
        both = jnp.dot(hot, jnp.concatenate([high, low], axis=1), preferred_element_type=F32)
        return both[:, :blk] + both[:, blk:]

    def hots(lo):
        hot = [jnp.where(vox_row == in_lists[k, 0:1, :], 1.0, 0.0).astype(BF16) for k in range(lo, lo + 4)]
        return jnp.concatenate(hot, axis=1)

    widen(0, q_near[0])

    def near_back(j, _):
        @at_step(j, 1)
        def _():
            around[1].wait_recv()
            around[3].wait_recv()
            widen(1, q_near[1])
            widen(3, q_near[3])

        @at_step(j, 3)
        def _():
            around[2].wait_recv()
            widen(2, q_near[2])

        back_products(turn(j))
        return 0

    lax.fori_loop(0, 4, near_back, 0)
    for c in range(2):
        over[c].wait_recv()
        for k in (2, 1, 3):
            onward[k, c].start()
    widen(4, q_far[0])
    hot = hots(0)
    for r in range(8):
        back[pl.ds(r * blocks, blocks)] = scattered(hot, 0, r)

    def far_back(j, _):
        @at_step(j, 1)
        def _():
            for k, c in ((1, 0), (3, 0), (1, 1), (3, 1)):
                onward[k, c].wait_recv()
            widen(5, q_far[1])
            widen(7, q_far[3])

        @at_step(j, 3)
        def _():
            for c in range(2):
                onward[2, c].wait_recv()
            widen(6, q_far[2])

        back_products(4 + turn(j))
        return 0

    lax.fori_loop(0, 4, far_back, 0)
    hot = hots(4)

    def finish(r):
        back[pl.ds(r * blocks, blocks)] += scattered(hot, 4, r)

    finish(0)
    finish(7)
    vol_up[...] += primal_w[1, 2] * back[pl.ds(0, blocks)]
    vol_down[...] += primal_w[1, 0] * back[pl.ds(7 * blocks, blocks)]
    to_next = remote(vol_down, back_prev, vs.at[0], vr.at[0], following)
    to_prev = remote(vol_up, back_next, vs.at[1], vr.at[1], prev)

    @pl.when(has_next)
    def _():
        to_next.start()

    @pl.when(has_prev)
    def _():
        to_prev.start()

    for r in range(1, 7):
        finish(r)

    for r in range(8):
        value = primal_w[1, 1] * back[pl.ds(r * blocks, blocks)]
        if r > 0:
            value = value + primal_w[1, 0] * back[pl.ds((r - 1) * blocks, blocks)]
        if r < 7:
            value = value + primal_w[1, 2] * back[pl.ds((r + 1) * blocks, blocks)]
        terms[pl.ds(r * (blocks + 8), blocks)] = value

    @pl.when(has_prev)
    def _():
        to_next.wait_recv()
        terms[pl.ds(0, blocks)] += back_prev[...]

    @pl.when(has_next)
    def _():
        to_prev.wait_recv()
        terms[pl.ds(7 * (blocks + 8), blocks)] += back_next[...]

    def merge(i, _):
        for u in range(16):
            v = i * 16 + u
            new_vol[v] += terms[pl.ds(v, 8, stride=blocks + 8), :]
        return 0

    lax.fori_loop(0, blocks // 16, merge, 0)

    sent = [list_copies, near_copies, far_copies, around, onward]
    for copy in [copy for group_of in sent for copy in group_of.values()] + [across] + over:
        copy.wait_send()

    @pl.when(has_prev)
    def _():
        far_up.wait_send()
        near_up.wait_send()
        to_prev.wait_send()

    @pl.when(has_next)
    def _():
        far_down.wait_send()
        near_down.wait_send()
        to_next.wait_send()


def store_kernel(vol_ref, dual_ref, vol_out, dual_out, sem):
    copies = [
        pltpu.make_async_copy(source, target, sem.at[i])
        for i, (source, target) in enumerate([(vol_ref, vol_out), (dual_ref, dual_out)])
    ]
    for copy in copies:
        copy.start()
    for copy in copies:
        copy.wait()


def on_device(volume, dual, measured, tiles, lists, live, dual_kernel, primal_kernel):
    groups, slabs = lax.axis_size("angle"), lax.axis_size("slab")
    blocks, _, blk = volume.shape
    width = dual.shape[2]
    det = width // blk
    rows = det * 8
    vmem, smem = pl.BlockSpec(memory_space=pltpu.VMEM), pl.BlockSpec(memory_space=pltpu.SMEM)
    hbm = pl.BlockSpec(memory_space=pl.ANY)
    dma = pltpu.SemaphoreType.DMA
    ramp = jnp.asarray(ramp_matrix(width, blk))
    outs = pl.pallas_call(
        functools.partial(step_kernel, slabs),
        out_shape=[pltpu.VMEM(volume.shape, F32), pltpu.VMEM((8, width), F32)],
        in_specs=[hbm] * 9,
        out_specs=[vmem, vmem],
        scratch_shapes=[
            pltpu.VMEM(lists.shape, jnp.int32),
            pltpu.SMEM(live.shape, jnp.int32),
            pltpu.SMEM(dual_kernel.shape, F32),
            pltpu.SMEM(primal_kernel.shape, F32),
            pltpu.VMEM(volume.shape, F32),
            pltpu.VMEM((8, width), F32),
            pltpu.VMEM((8, width), F32),
            pltpu.VMEM(tiles.shape, BF16),
            pltpu.VMEM(ramp.shape, BF16),
            pltpu.VMEM((tiles.shape[0] * blocks, 8, blk), F32),
            pltpu.VMEM((blocks * 8, blk), BF16),
            pltpu.VMEM((groups, 8, blk), jnp.int32),
            pltpu.VMEM((groups, 8, blk), jnp.int32),
            pltpu.VMEM((groups, 8, blk), jnp.int32),
            pltpu.SMEM((groups, 8, blk), jnp.int32),
            pltpu.VMEM((10 * blk, blk), F32),
            pltpu.VMEM((10 * blk, blk), F32),
            pltpu.VMEM((8, rows, blk), BF16),
            pltpu.VMEM((3, rows, blk), BF16),
            pltpu.VMEM((3, rows, blk), BF16),
            pltpu.VMEM((rows + det, blk), F32),
            pltpu.VMEM((rows, blk), BF16),
            pltpu.VMEM((rows, blk), BF16),
            pltpu.VMEM((8, width), F32),
        ]
        + [pltpu.VMEM((1, width), F32)] * 4
        + [pltpu.VMEM((det, blk), BF16)] * 2
        + [pltpu.VMEM((2 * rows, blk), BF16)] * 4
        + [pltpu.VMEM((4, rows, blk), BF16)] * 2
        + [
            pltpu.VMEM((groups * (det + 1), 8, blk), F32),
            pltpu.VMEM((9 * (groups * blk + 8), blk), F32),
            pltpu.VMEM((8 * blocks, blk), F32),
        ]
        + [pltpu.VMEM((blocks, blk), F32)] * 4
        + [dma((4,)), dma((5,)), dma((7,)), dma((7,)), dma((8,))]
        + [dma((3,))] * 4
        + [dma((1,))] * 2
        + [dma((2,))] * 6
        + [dma((3,))] * 2
        + [dma((3, 2))] * 2
        + [dma((2,))] * 2,
        compiler_params=pltpu.CompilerParams(
            collective_id=0, has_side_effects=True, vmem_limit_bytes=VMEM_LIMIT
        ),
    )(lists, live, volume, dual[0], measured[0], tiles, ramp, dual_kernel, primal_kernel)
    new_volume, new_dual = pl.pallas_call(
        store_kernel,
        out_shape=[jax.ShapeDtypeStruct(volume.shape, F32), jax.ShapeDtypeStruct((8, width), F32)],
        in_specs=[vmem, vmem],
        out_specs=[hbm, hbm],
        scratch_shapes=[dma((2,))],
    )(*[pltpu.with_memory_space_constraint(out, pltpu.VMEM) for out in outs])
    return (new_volume, new_dual[None])


def solution(mesh):
    in_specs = (
        P("angle", "slab", None),
        P("angle", "slab", None),
        P("angle", "slab", None),
        P(),
        P(None, "slab", "angle"),
        P("slab", "angle"),
        P(),
        P(),
    )
    out_specs = (P("angle", "slab", None), P("angle", "slab", None))
    return jax.shard_map(
        on_device, mesh=mesh, in_specs=in_specs, out_specs=out_specs, check_vma=False
    )
```

```python
import functools

import jax
import jax.numpy as jnp
import ml_dtypes
import numpy as np
from jax import lax
from jax.experimental import pallas as pl
from jax.experimental.pallas import tpu as pltpu
from jax.sharding import PartitionSpec as P

F32 = jnp.float32
BF16 = jnp.bfloat16
MESH = pl.DeviceIdType.MESH
CONTRACT_LAST = (((1,), (1,)), ((), ()))
CONTRACT_INNER = (((1,), (0,)), ((), ()))
VMEM_LIMIT = 56 * 2**20
X_SIZE = 4


def ramp_matrix(width, blk):
    n = np.arange(width)
    taps = np.zeros(width)
    odd = n % 2 == 1
    taps[odd] = -(2.0 / width**2) / np.sin(np.pi * n[odd] / width) ** 2
    k = np.arange(width // blk)[:, None, None]
    i = np.arange(blk)[None, :, None]
    j = np.arange(blk)[None, None, :]
    full = taps[(blk * k + j - i) % width].reshape(width, blk)
    high = full.astype(ml_dtypes.bfloat16)
    low = (full - high.astype(np.float64)).astype(ml_dtypes.bfloat16)
    return np.concatenate([high, low], axis=1)


def remote(src, dst, send, recv, device):
    return pltpu.make_async_remote_copy(
        src_ref=src, dst_ref=dst, send_sem=send, recv_sem=recv, device_id=device, device_id_type=MESH
    )


def step_kernel(
    slabs,
    lists_hbm,
    live_hbm,
    vol_hbm,
    dual_hbm,
    meas_hbm,
    tiles_hbm,
    ramp_hbm,
    dual_w_hbm,
    primal_w_hbm,
    new_vol,
    new_dual,
    lists_ref,
    live_ref,
    dual_w,
    primal_w,
    vol_ref,
    dual_ref,
    meas_ref,
    tiles,
    ramp,
    dense,
    rounded,
    out_lists,
    in_lists,
    prepared,
    index,
    picked,
    picked_too,
    part,
    land_near,
    land_far,
    near,
    send_z,
    land_z,
    misfit,
    down,
    up,
    from_prev,
    from_next,
    far_prev,
    far_next,
    even,
    odd,
    even_low,
    odd_low,
    q_near,
    q_far,
    wide,
    terms,
    back,
    vol_down,
    vol_up,
    back_prev,
    back_next,
    small_sem,
    load_sem,
    ls,
    lr,
    index_sem,
    ns,
    nr,
    fs,
    fr,
    zs,
    zr,
    es,
    er,
    ps,
    pr,
    gs,
    gr,
    hs,
    hr,
    ws,
    wr,
    vs,
    vr,
):
    slab, me = lax.axis_index("slab"), lax.axis_index("angle")
    x, z = me // 2, lax.rem(me, 2)
    has_prev, has_next = slab > 0, slab < slabs - 1
    blocks, _, blk = vol_ref.shape
    width = dual_ref.shape[1]
    det = width // blk
    rows = det * 8
    seg = blk
    pairs = 8 * seg
    tile_count = tiles.shape[0]

    def group(k):
        return 2 * lax.rem(x + k % 4, 4) + (1 - z if k >= 4 else z)

    def device(k):
        return (slab, group(k))

    def mirror(k):
        return (4 - k % 4) % 4 + 4 * (k // 4)

    prev, following = (slab - 1, me), (slab + 1, me)
    far_me = 2 * x + 1 - z
    prev_far, following_far = (slab - 1, far_me), (slab + 1, far_me)

    barrier = pltpu.get_barrier_semaphore()
    for k in range(1, 8):
        pl.semaphore_signal(barrier, inc=1, device_id=device(k), device_id_type=MESH)

    @pl.when(has_prev)
    def _():
        pl.semaphore_signal(barrier, inc=1, device_id=prev, device_id_type=MESH)
        pl.semaphore_signal(barrier, inc=1, device_id=prev_far, device_id_type=MESH)

    @pl.when(has_next)
    def _():
        pl.semaphore_signal(barrier, inc=1, device_id=following, device_id_type=MESH)
        pl.semaphore_signal(barrier, inc=1, device_id=following_far, device_id_type=MESH)

    small = [
        pltpu.make_async_copy(source, target, small_sem.at[i])
        for i, (source, target) in enumerate(
            [(lists_hbm, lists_ref), (live_hbm, live_ref), (dual_w_hbm, dual_w), (primal_w_hbm, primal_w)]
        )
    ]
    for load in small:
        load.start()
    loads = [
        pltpu.make_async_copy(source, target, load_sem.at[i])
        for i, (source, target) in enumerate(
            [(tiles_hbm, tiles), (vol_hbm, vol_ref), (dual_hbm, dual_ref), (meas_hbm, meas_ref), (ramp_hbm, ramp)]
        )
    ]
    for load in loads:
        load.start()

    for load in small:
        load.wait()
    lane = lax.broadcasted_iota(jnp.int32, (1, seg), 1)
    for j in range(8):
        cols = pl.ds(j * seg, seg)
        out_lists[j, 0:1, :] = jnp.clip(lists_ref[0, :, cols] - j * blocks, 0, blocks - 1)
        out_lists[j, 1:2, :] = jnp.where(lane < live_ref[0, j], lists_ref[1, :, cols], det)
        out_lists[j, 2:3, :] = lists_ref[2, :, cols]
        out_lists[j, 3:8, :] = jnp.zeros((5, seg), jnp.int32)

    def prepare(k):
        voxel, detector, tile = in_lists[k, 0:1, :], in_lists[k, 1:2, :], in_lists[k, 2:3, :]
        prepared[k, 0:1, :] = tile * blocks + voxel
        prepared[k, 1:2, :] = detector + k * (det + 1)
        prepared[k, 2:8, :] = in_lists[k, 2:8, :]
        copy = pltpu.make_async_copy(prepared.at[k], index.at[k], index_sem.at[k])
        copy.start()
        return copy

    in_lists[0] = out_lists[me]
    own_index = prepare(0)
    loads[0].wait()
    loads[1].wait()
    rounded[...] = vol_ref[...].reshape(blocks * 8, blk).astype(BF16)

    def products(i, _):
        for u in range(0, 8, 2):
            t = i * 8 + u
            both = lax.dot_general(
                rounded[...], tiles[pl.ds(t, 2)].reshape(2 * blk, blk), CONTRACT_LAST, preferred_element_type=F32
            )
            dense[pl.ds(t * blocks, blocks)] = both[:, :blk].reshape(blocks, 8, blk)
            dense[pl.ds((t + 1) * blocks, blocks)] = both[:, blk:].reshape(blocks, 8, blk)
        return 0

    early = tile_count // 8 - 4
    lax.fori_loop(0, early, products, 0)
    present = 2 * (has_prev.astype(jnp.int32) + has_next.astype(jnp.int32))
    pl.semaphore_wait(barrier, 7 + present)

    list_copies = {}
    for k in (6, 5, 7, 4, 2, 1, 3):
        list_copies[k] = remote(
            out_lists.at[group(k)], in_lists.at[mirror(k)], ls.at[k - 1], lr.at[mirror(k) - 1], device(k)
        )
        list_copies[k].start()
    lax.fori_loop(early, tile_count // 8, products, 0)

    def split(value):
        high = value.astype(BF16)
        return high, (value - high.astype(F32)).astype(BF16)

    det_row = lax.broadcasted_iota(jnp.int32, (det, seg), 0)

    sides = (picked, picked_too)

    def project(k, side, after=None):
        parts = []
        for r in range(8):
            if after is not None:
                for i in range(r * seg // 8, (r + 1) * seg // 8):
                    sides[1 - side][pl.ds(i, 8, stride=seg + 8), :] = dense[index[after, 0, i]]
            if k is not None:
                parts.append(split(sides[side][pl.ds(r * (seg + 8), seg)]))
        if k is None:
            return
        stacked = jnp.concatenate(
            [jnp.concatenate([p[0] for p in parts], axis=1), jnp.concatenate([p[1] for p in parts], axis=1)], axis=0
        )
        hot = jnp.where(det_row == in_lists[k, 1:2, :], 1.0, 0.0).astype(BF16)
        summed = jnp.dot(jnp.concatenate([hot, hot], axis=1), stacked, preferred_element_type=F32)
        for r in range(8):
            here = pl.ds(r * det, det)
            value = summed[:, r * blk : (r + 1) * blk]
            if k == 0:
                near[here] = value
            else:
                part[k, here] = value.astype(BF16)

    def turn(j):
        return lax.rem(j * (j + 1) // 2, 4)

    near_copies = {
        d: remote(part.at[d], land_near.at[mirror(d) - 1], ns.at[d - 1], nr.at[mirror(d) - 1], device(d))
        for d in (1, 3, 2)
    }
    far_copies = {
        d: remote(part.at[d + 4], land_far.at[mirror(d) - 1], fs.at[d - 1], fr.at[mirror(d) - 1], device(d))
        for d in (2, 3, 1)
    }

    def at_step(j, step):
        return pl.when(j == step)

    def receive(ks):
        for k in ks:
            list_copies[k].wait_recv()
        copies = [prepare(k) for k in ks]
        for copy in copies:
            copy.wait()

    own_index.wait()
    project(None, 1, 0)
    receive((1, 3, 2))
    project(0, 0, 1)
    project(1, 1, 3)
    near_copies[1].start()
    project(3, 0, 2)
    near_copies[3].start()
    project(2, 1)
    near_copies[2].start()
    receive((4, 5, 7, 6))
    project(None, 1, 6)
    project(6, 0, 7)
    far_copies[2].start()
    project(7, 1, 5)
    far_copies[3].start()
    project(5, 0, 4)
    far_copies[1].start()
    project(4, 1)

    for copy in far_copies.values():
        copy.wait_recv()
    total = part[4].astype(F32)
    for d in range(3):
        total = total + land_far[d].astype(F32)
    send_z[...] = total.astype(BF16)
    across = remote(send_z, land_z, zs.at[0], zr.at[0], device(4))
    across.start()
    first, last = pl.ds(0, det), pl.ds(rows - det, det)
    far_up = remote(send_z.at[first], far_next, ps.at[0], pr.at[0], prev_far)
    far_down = remote(send_z.at[last], far_prev, ps.at[1], pr.at[1], following_far)

    @pl.when(has_prev)
    def _():
        far_up.start()

    @pl.when(has_next)
    def _():
        far_down.start()

    loads[2].wait()
    loads[3].wait()
    for copy in near_copies.values():
        copy.wait_recv()
    whole = pl.ds(0, rows)
    total = near[whole]
    for d in range(3):
        total = total + land_near[d].astype(F32)
    near[whole] = total
    for b in range(det):
        cols = pl.ds(b * blk, blk)
        misfit[:, cols] = near[pl.ds(b, 8, stride=det), :] - meas_ref[:, cols]
    down[...] = dual_w[0, 0] * dual_ref[7:8, :] + dual_w[1, 0] * misfit[7:8, :]
    up[...] = dual_w[0, 2] * dual_ref[0:1, :] + dual_w[1, 2] * misfit[0:1, :]
    near_down = remote(down, from_prev, es.at[0], er.at[0], following)
    near_up = remote(up, from_next, es.at[1], er.at[1], prev)

    @pl.when(has_next)
    def _():
        near_down.start()

    @pl.when(has_prev)
    def _():
        near_up.start()

    vol_down[...] = vol_ref[:, 7, :] * primal_w[0, 0]
    vol_up[...] = vol_ref[:, 0, :] * primal_w[0, 2]
    for k in range(8):
        wide[k * (det + 1) + det] = jnp.zeros((8, blk), F32)
    row = lax.broadcasted_iota(jnp.int32, (1, 8, blk), 1)

    def volume_part(i, _):
        here = pl.ds(i * 8, 8)
        vol = vol_ref[here]
        before = jnp.where(row == 0, 0.0, pltpu.roll(primal_w[0, 0] * vol, 1, 1))
        after = jnp.where(row == 7, 0.0, pltpu.roll(primal_w[0, 2] * vol, 7, 1))
        new_vol[here] = vol + primal_w[0, 1] * vol + before + after
        return 0

    lax.fori_loop(0, blocks // 8, volume_part, 0)
    loads[4].wait()

    @pl.when(has_prev)
    def _():
        near_down.wait_recv()
        far_down.wait_recv()

    @pl.when(jnp.logical_not(has_prev))
    def _():
        from_prev[...] = jnp.zeros_like(from_prev)
        far_prev[...] = jnp.zeros_like(far_prev)

    @pl.when(has_next)
    def _():
        near_up.wait_recv()
        far_up.wait_recv()

    @pl.when(jnp.logical_not(has_next))
    def _():
        from_next[...] = jnp.zeros_like(from_next)
        far_next[...] = jnp.zeros_like(far_next)

    across.wait_recv()
    near[whole] = land_z[...].astype(F32)
    flat_row = lax.broadcasted_iota(jnp.int32, (8, blk), 0)
    before_far = far_prev[...].astype(F32) * dual_w[1, 0]
    after_far = far_next[...].astype(F32) * dual_w[1, 2]

    def updated(b):
        cols = pl.ds(b * blk, blk)
        dual = dual_ref[:, cols]
        mis = misfit[:, cols] + near[pl.ds(b, 8, stride=det), :]
        before = pltpu.roll(dual_w[0, 0] * dual + dual_w[1, 0] * mis, 1, 0)
        after = pltpu.roll(dual_w[0, 2] * dual + dual_w[1, 2] * mis, 7, 0)
        before = jnp.where(flat_row == 0, from_prev[:, cols] + before_far[b : b + 1], before)
        after = jnp.where(flat_row == 7, from_next[:, cols] + after_far[b : b + 1], after)
        new = dual + dual_w[0, 1] * dual + dual_w[1, 1] * mis + before + after
        new_dual[:, cols] = new
        return new

    news = [updated(b) for b in range(det)]
    for b in range(det):
        high, low = split(jnp.concatenate([news[b], news[(b + 1) % det]], axis=0))
        for base in (0, rows):
            if b % 2 == 0:
                even[pl.ds(base + b * 8, 16)] = high
                even_low[pl.ds(base + b * 8, 16)] = low
            else:
                odd[pl.ds(base + (b - 1) * 8, 16)] = high
                odd_low[pl.ds(base + (b - 1) * 8, 16)] = low
    total = jnp.zeros((rows, 2 * blk), F32)
    small = jnp.zeros((rows, blk), F32)
    for k in range(0, det, 2):
        here = pl.ds((det - k) * 8 % rows, rows)
        there = pl.ds((det - k - 2) * 8, rows)
        weight = ramp[pl.ds(k * blk, 2 * blk)]
        high = jnp.concatenate([even[here], odd[there]], axis=1)
        low = jnp.concatenate([even_low[here], odd_low[there]], axis=1)
        total = total + jnp.dot(high, weight, preferred_element_type=F32)
        small = small + jnp.dot(low, weight[:, :blk], preferred_element_type=F32)
    small = small + total[:, blk:] + total[:, :blk]
    for b in range(0, det, 2):
        both = jnp.concatenate([new_dual[:, pl.ds(b * blk, blk)], new_dual[:, pl.ds((b + 1) * blk, blk)]], axis=0)
        q_near[0, pl.ds(b * 8, 16)] = (0.5 * both + small[b * 8 : b * 8 + 16]).astype(BF16)

    step = rows // 2
    halves = [pl.ds(0, step), pl.ds(step, step)]
    over = []
    for c, half in enumerate(halves):
        over.append(remote(q_near.at[0, half], q_far.at[0, half], gs.at[c], gr.at[c], device(4)))
        over[c].start()
    around, onward = {}, {}
    for k in (2, 1, 3):
        around[k] = remote(q_near.at[0], q_near.at[mirror(k)], hs.at[k - 1], hr.at[mirror(k) - 1], device(k))
        around[k].start()
        for c, half in enumerate(halves):
            onward[k, c] = remote(
                q_far.at[0, half], q_far.at[mirror(k), half], ws.at[k - 1, c], wr.at[mirror(k) - 1, c], device(k)
            )

    def widen(k, value):
        wide[pl.ds(k * (det + 1), det)] = value.reshape(det, 8, blk).astype(F32)

    def back_products(k):
        for i in range(0, seg, 2):
            left = jnp.concatenate([wide[index[k, 1, i]], wide[index[k, 1, i + 1]]], axis=0).astype(BF16)
            weight = jnp.concatenate([tiles[index[k, 2, i]], tiles[index[k, 2, i + 1]]], axis=1)
            both = jnp.dot(left, weight, preferred_element_type=F32)
            p = k * seg + i
            terms[pl.ds(p, 8, stride=pairs + 8), :] = both[:8, :blk]
            terms[pl.ds(p + 1, 8, stride=pairs + 8), :] = both[8:, blk:]

    vox_row = lax.broadcasted_iota(jnp.int32, (blocks, seg), 0)

    def scattered(hot, lo, r):
        high, low = split(terms[pl.ds(r * (pairs + 8) + lo * seg, 4 * seg)])
        both = jnp.dot(hot, jnp.concatenate([high, low], axis=1), preferred_element_type=F32)
        return both[:, :blk] + both[:, blk:]

    def hots(lo):
        hot = [jnp.where(vox_row == in_lists[k, 0:1, :], 1.0, 0.0).astype(BF16) for k in range(lo, lo + 4)]
        return jnp.concatenate(hot, axis=1)

    widen(0, q_near[0])

    def near_back(j, _):
        @at_step(j, 1)
        def _():
            around[1].wait_recv()
            around[3].wait_recv()
            widen(1, q_near[1])
            widen(3, q_near[3])

        @at_step(j, 3)
        def _():
            around[2].wait_recv()
            widen(2, q_near[2])

        back_products(turn(j))
        return 0

    lax.fori_loop(0, 4, near_back, 0)
    for c in range(2):
        over[c].wait_recv()
        for k in (1, 3, 2):
            onward[k, c].start()
    widen(4, q_far[0])
    hot = hots(0)
    for r in range(8):
        back[pl.ds(r * blocks, blocks)] = scattered(hot, 0, r)

    def far_back(j, _):
        @at_step(j, 1)
        def _():
            for k, c in ((1, 0), (3, 0), (1, 1), (3, 1)):
                onward[k, c].wait_recv()
            widen(5, q_far[1])
            widen(7, q_far[3])

        @at_step(j, 3)
        def _():
            for c in range(2):
                onward[2, c].wait_recv()
            widen(6, q_far[2])

        back_products(4 + turn(j))
        return 0

    lax.fori_loop(0, 4, far_back, 0)
    hot = hots(4)

    def finish(r):
        back[pl.ds(r * blocks, blocks)] += scattered(hot, 4, r)

    finish(0)
    finish(7)
    vol_up[...] += primal_w[1, 2] * back[pl.ds(0, blocks)]
    vol_down[...] += primal_w[1, 0] * back[pl.ds(7 * blocks, blocks)]
    to_next = remote(vol_down, back_prev, vs.at[0], vr.at[0], following)
    to_prev = remote(vol_up, back_next, vs.at[1], vr.at[1], prev)

    @pl.when(has_next)
    def _():
        to_next.start()

    @pl.when(has_prev)
    def _():
        to_prev.start()

    for r in range(1, 7):
        finish(r)

    for r in range(8):
        value = primal_w[1, 1] * back[pl.ds(r * blocks, blocks)]
        if r > 0:
            value = value + primal_w[1, 0] * back[pl.ds((r - 1) * blocks, blocks)]
        if r < 7:
            value = value + primal_w[1, 2] * back[pl.ds((r + 1) * blocks, blocks)]
        terms[pl.ds(r * (blocks + 8), blocks)] = value

    @pl.when(has_prev)
    def _():
        to_next.wait_recv()
        terms[pl.ds(0, blocks)] += back_prev[...]

    @pl.when(has_next)
    def _():
        to_prev.wait_recv()
        terms[pl.ds(7 * (blocks + 8), blocks)] += back_next[...]

    def merge(i, _):
        for u in range(16):
            v = i * 16 + u
            new_vol[v] += terms[pl.ds(v, 8, stride=blocks + 8), :]
        return 0

    lax.fori_loop(0, blocks // 16, merge, 0)

    sent = [list_copies, near_copies, far_copies, around, onward]
    for copy in [copy for group_of in sent for copy in group_of.values()] + [across] + over:
        copy.wait_send()

    @pl.when(has_prev)
    def _():
        far_up.wait_send()
        near_up.wait_send()
        to_prev.wait_send()

    @pl.when(has_next)
    def _():
        far_down.wait_send()
        near_down.wait_send()
        to_next.wait_send()


def store_kernel(vol_ref, dual_ref, vol_out, dual_out, sem):
    copies = [
        pltpu.make_async_copy(source, target, sem.at[i])
        for i, (source, target) in enumerate([(vol_ref, vol_out), (dual_ref, dual_out)])
    ]
    for copy in copies:
        copy.start()
    for copy in copies:
        copy.wait()


def on_device(volume, dual, measured, tiles, lists, live, dual_kernel, primal_kernel):
    groups, slabs = lax.axis_size("angle"), lax.axis_size("slab")
    blocks, _, blk = volume.shape
    width = dual.shape[2]
    det = width // blk
    rows = det * 8
    vmem, smem = pl.BlockSpec(memory_space=pltpu.VMEM), pl.BlockSpec(memory_space=pltpu.SMEM)
    hbm = pl.BlockSpec(memory_space=pl.ANY)
    dma = pltpu.SemaphoreType.DMA
    ramp = jnp.asarray(ramp_matrix(width, blk))
    outs = pl.pallas_call(
        functools.partial(step_kernel, slabs),
        out_shape=[pltpu.VMEM(volume.shape, F32), pltpu.VMEM((8, width), F32)],
        in_specs=[hbm] * 9,
        out_specs=[vmem, vmem],
        scratch_shapes=[
            pltpu.VMEM(lists.shape, jnp.int32),
            pltpu.SMEM(live.shape, jnp.int32),
            pltpu.SMEM(dual_kernel.shape, F32),
            pltpu.SMEM(primal_kernel.shape, F32),
            pltpu.VMEM(volume.shape, F32),
            pltpu.VMEM((8, width), F32),
            pltpu.VMEM((8, width), F32),
            pltpu.VMEM(tiles.shape, BF16),
            pltpu.VMEM(ramp.shape, BF16),
            pltpu.VMEM((tiles.shape[0] * blocks, 8, blk), F32),
            pltpu.VMEM((blocks * 8, blk), BF16),
            pltpu.VMEM((groups, 8, blk), jnp.int32),
            pltpu.VMEM((groups, 8, blk), jnp.int32),
            pltpu.VMEM((groups, 8, blk), jnp.int32),
            pltpu.SMEM((groups, 8, blk), jnp.int32),
            pltpu.VMEM((10 * blk, blk), F32),
            pltpu.VMEM((10 * blk, blk), F32),
            pltpu.VMEM((8, rows, blk), BF16),
            pltpu.VMEM((3, rows, blk), BF16),
            pltpu.VMEM((3, rows, blk), BF16),
            pltpu.VMEM((rows + det, blk), F32),
            pltpu.VMEM((rows, blk), BF16),
            pltpu.VMEM((rows, blk), BF16),
            pltpu.VMEM((8, width), F32),
        ]
        + [pltpu.VMEM((1, width), F32)] * 4
        + [pltpu.VMEM((det, blk), BF16)] * 2
        + [pltpu.VMEM((2 * rows, blk), BF16)] * 4
        + [pltpu.VMEM((4, rows, blk), BF16)] * 2
        + [
            pltpu.VMEM((groups * (det + 1), 8, blk), F32),
            pltpu.VMEM((9 * (groups * blk + 8), blk), F32),
            pltpu.VMEM((8 * blocks, blk), F32),
        ]
        + [pltpu.VMEM((blocks, blk), F32)] * 4
        + [dma((4,)), dma((5,)), dma((7,)), dma((7,)), dma((8,))]
        + [dma((3,))] * 4
        + [dma((1,))] * 2
        + [dma((2,))] * 6
        + [dma((3,))] * 2
        + [dma((3, 2))] * 2
        + [dma((2,))] * 2,
        compiler_params=pltpu.CompilerParams(
            collective_id=0, has_side_effects=True, vmem_limit_bytes=VMEM_LIMIT
        ),
    )(lists, live, volume, dual[0], measured[0], tiles, ramp, dual_kernel, primal_kernel)
    new_volume, new_dual = pl.pallas_call(
        store_kernel,
        out_shape=[jax.ShapeDtypeStruct(volume.shape, F32), jax.ShapeDtypeStruct((8, width), F32)],
        in_specs=[vmem, vmem],
        out_specs=[hbm, hbm],
        scratch_shapes=[dma((2,))],
    )(*[pltpu.with_memory_space_constraint(out, pltpu.VMEM) for out in outs])
    return (new_volume, new_dual[None])


def solution(mesh):
    in_specs = (
        P("angle", "slab", None),
        P("angle", "slab", None),
        P("angle", "slab", None),
        P(),
        P(None, "slab", "angle"),
        P("slab", "angle"),
        P(),
        P(),
    )
    out_specs = (P("angle", "slab", None), P("angle", "slab", None))
    return jax.shard_map(
        on_device, mesh=mesh, in_specs=in_specs, out_specs=out_specs, check_vma=False
    )
```
